128 devices in a mesh: row: 16 (over z, y_lo, core), col: 8 (over x, y_hi).
Axes of the slice: x: 4, y: 4 (y_hi: 2, y_lo: 2; y = y_hi * 2 + y_lo), z: 4, core: 2. Of those that a mesh axis runs over, the one named last changes fastest.
Arguments:
- amplitudes: bfloat16 [80, 80, 128, 128], P('row'), may hold values from -6 to 6
- integrals: bfloat16 [80, 80, 128, 128], P('row', 'col'), may hold values from -0.078125 to 0.078125
- pair_lists: int32 [80, 80, 48], P('row', 'col'), may hold values from 0 to 79, as said below
- pair_counts: int32 [80, 80], P('row', 'col'), may hold values from 24 to 48, as said below
Outputs:
- residual: float32 [80, 80, 128, 128], P('row', 'col')
The draws below stay inside these ranges and needn't reach their ends.
Inputs may be any that keep to these rules, and one draw needn't show every extreme that they name: `pair_lists`: the 48 entries of each pair's list are distinct. `pair_counts`: every diagonal pair (i, i) keeps all 48 entries.
All inputs are finite; a program needn't handle non-finite values.
Results may differ from the reference program's by a relative error of at most 0.0003.
Values may be sent and summed in bfloat16 or wider, within the bound.
A program may use at most 64 MiB of HBM per device.

```python
import jax
import jax.numpy as jnp
from jax import lax

O = 80
TILE = 128
NL = 48


def draw_pair_lists(key, part):
    key = jax.random.fold_in(key, 11)
    scores = jax.random.randint(key, (O, O, O), 0, 2 ** 20) * 128 + jnp.arange(O, dtype=jnp.int32)
    ordered = jnp.argsort(scores, axis=-1, stable=True)
    return ordered[:, :, :NL].astype(jnp.int32)


def draw_pair_counts(key, part):
    key = jax.random.fold_in(key, 23)
    counts_drawn = jax.random.randint(key, (O, O), NL // 2, NL + 1)
    diagonal = jnp.arange(O)[:, None] == jnp.arange(O)[None, :]
    return jnp.where(diagonal, NL, counts_drawn).astype(jnp.int32)


def block_levels(key, shape, split, smallest, high):
    gain = 1.0
    for position, blocks in split:
        draws = jax.random.uniform(jax.random.fold_in(jax.random.fold_in(key, 6), position), (blocks,), jnp.float32, smallest / len(split), high / len(split))
        gain = gain * jnp.repeat(jnp.exp(draws), shape[position] // blocks).reshape((-1,) + (1,) * (len(shape) - 1 - position))
    return gain


def gaussian(key, dims, width, most, cuts=(), held_as=jnp.bfloat16):
    gain = block_levels(key, dims, cuts, -0.22, 0.18) if cuts else 1.0
    values = jax.random.normal(key, dims, jnp.float32) * width * gain
    return jnp.minimum(jnp.maximum(values, -most), most).astype(held_as)


def setup_inputs(seed: int = 0) -> dict:
    key_list = jax.random.split(jax.random.key(seed), 5)
    return {
        "amplitudes": gaussian(key_list[0], (O, O, TILE, TILE), 1.0, 6.0, ((0, 16),)),
        "integrals": gaussian(key_list[1], (O, O, TILE, TILE), (TILE * NL) ** -0.5, 0.078125, ((0, 16), (1, 8))),
        "pair_lists": draw_pair_lists(jax.random.fold_in(key_list[4], 71), 0),
        "pair_counts": draw_pair_counts(jax.random.fold_in(key_list[4], 71), 0),
    }


def reference(amplitudes, integrals, pair_lists, pair_counts):
    k_labels = jnp.arange(O, dtype=jnp.int32)
    slot_ids = jnp.arange(NL, dtype=jnp.int32)
    wide_integrals = integrals.astype(jnp.float32)

    def one_row(packed):
        amp_row, kept_list, kept_count = packed
        matches = (kept_list[:, :, None] == k_labels[None, None, :]) & (slot_ids[None, :, None] < kept_count[:, None, None])
        alive_mask = jnp.any(matches, axis=1).astype(jnp.bfloat16)
        masked = (amp_row[None, :, :, :] * alive_mask[:, :, None, None]).astype(jnp.float32)
        return jnp.einsum('jkac,kjcb->jab', masked, wide_integrals)

    contracted = lax.map(one_row, (amplitudes, pair_lists, pair_counts))
    return contracted + jnp.transpose(contracted, (1, 0, 3, 2))
```

```python
import functools

import jax
import jax.numpy as jnp
from jax import lax
from jax.experimental import pallas as pl
from jax.experimental.pallas import tpu as pltpu
from jax.sharding import PartitionSpec as P

MESH = pl.DeviceIdType.MESH
TILE = 128
O = 80
HALF = 5
CHIP = 10
GROUPS = ((0, 1), (2, 3), (4,))
Y, BACK, FRONT, FAR, BACK_Y, FRONT_Y, FAR_Y = range(7)


def kernel(
    amp, integ, mask, direct, mirror,
    tv, wv, cyc, cyct, mv, ms,
    own_sem, pair_send, pair_recv, t_own, t_send, t_recv, m_sem,
    g_send, g_recv, d_own, d_send, d_recv, x_send, x_recv,
):
    row, col = lax.axis_index("row"), lax.axis_index("col")
    z, y, c = row // 4, (row // 2) % 2, row % 2
    chip = row // 2
    other = 1 - c
    sibling = (row + 1 - 2 * c, col)
    y_dev = (row + 2 - 4 * y, col)
    up = (lax.rem(row + 4, 16), col)
    down = (lax.rem(row + 12, 16), col)
    partner = (2 * col + c, chip)
    off_diagonal = chip != col

    def block(dz, dy):
        return lax.rem(z + dz + 4, 4) * 2 + (y if dy == 0 else 1 - y)

    barrier = pltpu.get_barrier_semaphore()
    for device in (sibling, y_dev, up, down):
        pl.semaphore_signal(barrier, inc=1, device_id=device, device_id_type=MESH)

    @pl.when(off_diagonal)
    def _():
        pl.semaphore_signal(barrier, inc=1, device_id=partner, device_id_type=MESH)
        pl.semaphore_wait(barrier, 5)

    @pl.when(jnp.logical_not(off_diagonal))
    def _():
        pl.semaphore_wait(barrier, 4)

    def remote(src, dst, send, recv, device):
        return pltpu.make_async_remote_copy(
            src_ref=src, dst_ref=dst, send_sem=send, recv_sem=recv, device_id=device, device_id_type=MESH
        )

    mine = pl.ds(chip * CHIP + c * HALF, HALF)
    theirs = pl.ds(chip * CHIP + other * HALF, HALF)
    own_w = [pltpu.make_async_copy(integ.at[:, c * HALF + j], wv.at[j, mine], own_sem.at[j]) for j in range(HALF)]
    pair_w = [
        remote(integ.at[:, other * HALF + j], wv.at[j, mine], pair_send.at[j], pair_recv.at[j], sibling)
        for j in range(HALF)
    ]
    for j in range(HALF):
        own_w[j].start()
        pair_w[j].start()

    mask_pair = remote(mask.at[other], mv, m_sem.at[0], m_sem.at[1], sibling)
    mask_pair.start()
    mask_own = pltpu.make_async_copy(mask.at[c], ms.at[c], m_sem.at[2])
    mask_own.start()

    def piece(kind, j, dz, dy):
        part = c if kind == 0 else other
        view = pl.ds(block(dz, dy) * CHIP + part * HALF, HALF)
        return wv.at[j, view]

    sends = []

    def send(kind, j, dz, dy, name, device):
        ref = piece(kind, j, dz, dy)
        slot = (j * 2 + kind) * 7 + name
        copy = remote(ref, ref, g_send.at[slot], g_recv.at[slot], device)
        copy.start()
        sends.append(copy)

    def arrived(kind, j, name):
        far = 1 if (kind + j) % 2 == 0 else -1
        dz, dy = {
            Y: (0, 1), BACK: (-far, 0), FRONT: (far, 0), FAR: (2, 0),
            BACK_Y: (-far, 1), FRONT_Y: (far, 1), FAR_Y: (2, 1),
        }[name]
        ref = piece(kind, j, dz, dy)
        slot = (j * 2 + kind) * 7 + name
        remote(ref, ref, g_send.at[slot], g_recv.at[slot], y_dev).wait_recv()

    def ahead(kind, j):
        plus = (kind + j) % 2 == 0
        return (up, down, 1) if plus else (down, up, -1)

    def stage0(j):
        for kind in range(2):
            front, back, far = ahead(kind, j)
            if kind == 0:
                own_w[j].wait()
            else:
                pair_w[j].wait_recv()
            send(kind, j, 0, 0, BACK, front)
            send(kind, j, 0, 0, FRONT, back)
            send(kind, j, 0, 0, Y, y_dev)

    def stage1(j):
        front, back, far = ahead(0, j)
        arrived(0, j, Y)
        send(0, j, 0, 1, BACK_Y, front)
        send(0, j, 0, 1, FRONT_Y, back)
        arrived(0, j, BACK)
        send(0, j, -far, 0, FAR, front)
        front, back, far = ahead(1, j)
        arrived(1, j, BACK)
        send(1, j, -far, 0, FAR, front)
        send(1, j, -far, 0, BACK_Y, y_dev)
        arrived(1, j, FRONT)
        send(1, j, far, 0, FRONT_Y, y_dev)

    def stage2(j):
        front, back, far = ahead(0, j)
        arrived(0, j, BACK_Y)
        send(0, j, -far, 1, FAR_Y, front)
        arrived(1, j, FAR)
        send(1, j, 2, 0, FAR_Y, y_dev)

    def near(j):
        arrived(0, j, FRONT)
        arrived(1, j, Y)

    def rest(j):
        for name in (FRONT_Y, FAR, FAR_Y):
            arrived(0, j, name)
        for name in (BACK_Y, FRONT_Y, FAR_Y):
            arrived(1, j, name)

    def contract(js, late):
        places = ((1, 1), (-1, 1), (2, 0), (2, 1)) if late else ((0, 0), (0, 1), (1, 0), (-1, 0))
        starts = [block(dz, dy) * CHIP for dz, dy in places]
        labels = [start + k for start in starts for k in range(CHIP)]

        def one(i, carry):
            left = jnp.concatenate([tv[i, k] for k in labels], axis=1)
            right = []
            for j in js:
                right.append(
                    jnp.concatenate(
                        [
                            wv[j, k] * jnp.full((TILE, TILE), ms[i // HALF, lax.rem(i, HALF) * HALF + j, k], jnp.float32).astype(jnp.bfloat16)
                            for k in labels
                        ],
                        axis=0,
                    )
                )
            right = right[0] if len(js) == 1 else jnp.concatenate(right, axis=1)
            out = jnp.dot(left, right, preferred_element_type=jnp.float32)
            for n, j in enumerate(js):
                tile = out[:, n * TILE : (n + 1) * TILE]
                if late:
                    tile = tile + cyc[j, i]
                    cyct[j, i] = tile.T
                cyc[j, i] = tile
            return carry

        lax.fori_loop(0, CHIP, one, 0)

    finals = []

    def hand_out(j):
        own = pltpu.make_async_copy(cyc.at[j, pl.ds(c * HALF, HALF)], direct.at[:, c * HALF + j], d_own.at[j])
        own.start()
        pair = remote(
            cyc.at[j, pl.ds(other * HALF, HALF)], direct.at[:, c * HALF + j], d_send.at[j], d_recv.at[j], sibling
        )
        pair.start()

        @pl.when(off_diagonal)
        def _():
            remote(cyct.at[j], mirror.at[j], x_send.at[j], x_recv.at[j], partner).start()

        @pl.when(jnp.logical_not(off_diagonal))
        def _():
            pltpu.make_async_copy(cyct.at[j], mirror.at[j], x_send.at[j]).start()

        finals.append((own, pair))

    t_local = [pltpu.make_async_copy(amp.at[i], tv.at[c * HALF + i], t_own.at[i]) for i in range(HALF)]
    t_pair = [remote(amp.at[i], tv.at[c * HALF + i], t_send.at[i], t_recv.at[i], sibling) for i in range(HALF)]

    stage0(0)
    for i in range(HALF):
        t_local[i].start()
        t_pair[i].start()
    stage0(1)
    stage1(0)
    stage0(2)
    stage1(1)
    stage2(0)
    stage0(3)
    stage1(2)
    stage2(1)
    near(0)
    near(1)
    mask_pair.wait()
    mask_own.wait()
    second = pltpu.make_async_copy(mv, ms.at[other], m_sem.at[2])
    second.start()
    second.wait()
    for i in range(HALF):
        t_local[i].wait()
        t_pair[i].wait()
    contract(GROUPS[0], False)
    stage0(4)
    stage1(3)
    stage2(2)
    rest(0)
    rest(1)
    contract(GROUPS[0], True)
    hand_out(0)
    hand_out(1)
    stage1(4)
    stage2(3)
    near(2)
    near(3)
    contract(GROUPS[1], False)
    stage2(4)
    rest(2)
    rest(3)
    contract(GROUPS[1], True)
    hand_out(2)
    hand_out(3)
    near(4)
    contract(GROUPS[2], False)
    rest(4)
    contract(GROUPS[2], True)
    hand_out(4)

    for copy in sends:
        copy.wait_send()
    for copy in pair_w:
        copy.wait_send()
    for own, pair in finals:
        own.wait()
        pair.wait()
    for j in range(HALF):
        @pl.when(off_diagonal)
        def _():
            remote(cyct.at[j], mirror.at[j], x_send.at[j], x_recv.at[j], partner).wait()

        @pl.when(jnp.logical_not(off_diagonal))
        def _():
            pltpu.make_async_copy(cyct.at[j], mirror.at[j], x_send.at[j]).wait()


def on_device(amplitudes, integrals, pair_lists, pair_counts):
    rows_here, cols_here, slots = pair_lists.shape
    in_count = jnp.arange(slots, dtype=jnp.int32)[None, None, :] < pair_counts[:, :, None]
    labels = jnp.arange(TILE, dtype=jnp.int32)
    live = jnp.any(
        (pair_lists[:, :, :, None] == labels[None, None, None, :]) & in_count[:, :, :, None], axis=2
    ).astype(jnp.float32)
    mask = live.reshape(rows_here, 2, HALF, TILE).transpose(1, 0, 2, 3).reshape(2, HALF * HALF, TILE)
    mask = jnp.pad(mask, ((0, 0), (0, 32 - HALF * HALF), (0, 0)))
    bf, f32 = jnp.bfloat16, jnp.float32
    dma = pltpu.SemaphoreType.DMA
    tiles = jax.ShapeDtypeStruct((HALF, CHIP, TILE, TILE), f32)
    anywhere = pl.BlockSpec(memory_space=pl.ANY)
    direct, mirror = pl.pallas_call(
        kernel,
        out_shape=(tiles, tiles),
        in_specs=[anywhere] * 3,
        out_specs=(anywhere, anywhere),
        scratch_shapes=[
            pltpu.VMEM((CHIP, O, TILE, TILE), bf),
            pltpu.VMEM((HALF, O, TILE, TILE), bf),
            pltpu.VMEM((HALF, CHIP, TILE, TILE), f32),
            pltpu.VMEM((HALF, CHIP, TILE, TILE), f32),
            pltpu.VMEM((32, TILE), f32),
            pltpu.SMEM((2, 32, TILE), f32),
            dma((HALF,)), dma((HALF,)), dma((HALF,)), dma((HALF,)), dma((HALF,)), dma((HALF,)), dma((3,)),
            dma((70,)), dma((70,)), dma((HALF,)), dma((HALF,)), dma((HALF,)), dma((HALF,)), dma((HALF,)),
        ],
        compiler_params=pltpu.CompilerParams(
            collective_id=0, has_side_effects=True, vmem_limit_bytes=60 * 1024 * 1024
        ),
        cost_estimate=pl.CostEstimate(flops=17_000_000_000, bytes_accessed=60_000_000, transcendentals=0),
    )(amplitudes, integrals, mask)
    return direct + mirror


def solution(mesh):
    placed = (
        P("row", None, None, None),
        P("row", "col", None, None),
        P("row", "col", None),
        P("row", "col"),
    )
    return jax.shard_map(
        on_device,
        mesh=mesh,
        in_specs=placed,
        out_specs=P("row", "col", None, None),
        check_vma=False,
    )
```

```python
import functools

import jax
import jax.numpy as jnp
from jax import lax
from jax.experimental import pallas as pl
from jax.experimental.pallas import tpu as pltpu
from jax.sharding import PartitionSpec as P

MESH = pl.DeviceIdType.MESH
TILE = 128
O = 80
HALF = 5
CHIP = 10
GROUPS = ((0, 1), (2, 3), (4,))
PACK = HALF * TILE + 16
TOP = 2.0**15
Y, BACK, FRONT, FAR, BACK_Y, FRONT_Y, FAR_Y = range(7)


def kernel(
    amp, integ, lists, counts, direct, mirror,
    tv, wv, cyc, code, via_y, via_z, mine_v, mv, ms,
    own_sem, pair_send, pair_recv, t_own, t_send, t_recv, m_sem,
    g_send, g_recv, d_own, d_send, d_recv,
    y_send, y_recv, z_send, z_recv, a_send, a_recv, b_send, b_recv, c_send,
):
    row, col = lax.axis_index("row"), lax.axis_index("col")
    z, y, c = row // 4, (row // 2) % 2, row % 2
    chip = row // 2
    other = 1 - c
    sibling = (row + 1 - 2 * c, col)
    y_dev = (row + 2 - 4 * y, col)
    up = (lax.rem(row + 4, 16), col)
    down = (lax.rem(row + 12, 16), col)
    x, y_hi = col // 2, col % 2
    delta = lax.rem(z - x + 4, 4)

    def at(px, lo, hi, pz):
        return (pz * 4 + lo * 2 + c, px * 2 + hi)

    crossing = y != y_hi
    diagonal = delta == 0
    turned = jnp.logical_not(diagonal)
    stays = jnp.logical_and(diagonal, jnp.logical_not(crossing))
    swapped = at(x, y_hi, y, z)
    flipped = at(z, y, y_hi, x)
    corner = at(x, y, y_hi, x)
    opposite = at(x, y, y_hi, lax.rem(z + 2, 4))

    def block(dz, dy):
        return lax.rem(z + dz + 4, 4) * 2 + (y if dy == 0 else 1 - y)

    barrier = pltpu.get_barrier_semaphore()

    def greet(device):
        pl.semaphore_signal(barrier, inc=1, device_id=device, device_id_type=MESH)

    for device in (sibling, y_dev, up, down):
        greet(device)

    @pl.when(crossing)
    def _():
        greet(swapped)

    @pl.when(turned)
    def _():
        greet(flipped)
        greet(at(z, y_hi, y, z))

    @pl.when(lax.rem(delta, 2) == 0)
    def _():
        greet(opposite)

    @pl.when(diagonal)
    def _():
        for step in range(1, 4):
            greet(at(lax.rem(x + step, 4), y_hi, y, z))

    peers = (
        4 + jnp.where(crossing, 1, 0) + jnp.where(turned, 2, 3) + jnp.where(lax.rem(delta, 2) == 0, 1, 0)
    )
    pl.semaphore_wait(barrier, peers)

    def remote(src, dst, send, recv, device):
        return pltpu.make_async_remote_copy(
            src_ref=src, dst_ref=dst, send_sem=send, recv_sem=recv, device_id=device, device_id_type=MESH
        )

    mine = pl.ds(chip * CHIP + c * HALF, HALF)
    theirs = pl.ds(chip * CHIP + other * HALF, HALF)
    own_w = [pltpu.make_async_copy(integ.at[:, c * HALF + j], wv.at[j, mine], own_sem.at[j]) for j in range(HALF)]
    pair_w = [
        remote(integ.at[:, other * HALF + j], wv.at[j, mine], pair_send.at[j], pair_recv.at[j], sibling)
        for j in range(HALF)
    ]
    for j in range(HALF):
        own_w[j].start()
        pair_w[j].start()

    mask_pair = remote(mine_v.at[other], mv, m_sem.at[0], m_sem.at[1], sibling)
    mask_own = pltpu.make_async_copy(mine_v.at[c], ms.at[c], m_sem.at[2])

    def make_mask():
        count_rows = counts[...]
        slots = lists.shape[2]
        eye = lax.broadcasted_iota(jnp.int32, (CHIP, CHIP), 0) == lax.broadcasted_iota(jnp.int32, (CHIP, CHIP), 1)
        slot_ids = lax.broadcasted_iota(jnp.int32, (CHIP, slots), 1)
        labels = lax.broadcasted_iota(jnp.int32, (CHIP, TILE), 1)
        for i in range(HALF):
            per_pair = jnp.broadcast_to(count_rows[i : i + 1], (CHIP, CHIP))
            count = jnp.sum(jnp.where(eye, per_pair, 0), axis=1, keepdims=True)
            kept = jnp.where(slot_ids < count, lists[i], -1)
            live = jnp.zeros((CHIP, TILE), jnp.float32)
            for s in range(slots):
                live = jnp.where(kept[:, s : s + 1] == labels, 1.0, live)
            for half in range(2):
                mine_v[half, i * 8 : i * 8 + HALF] = live[half * HALF : (half + 1) * HALF]

    def piece(kind, j, dz, dy):
        part = c if kind == 0 else other
        view = pl.ds(block(dz, dy) * CHIP + part * HALF, HALF)
        return wv.at[j, view]

    sends = []

    def send(kind, j, dz, dy, name, device):
        ref = piece(kind, j, dz, dy)
        slot = (j * 2 + kind) * 7 + name
        copy = remote(ref, ref, g_send.at[slot], g_recv.at[slot], device)
        copy.start()
        sends.append(copy)

    def arrived(kind, j, name):
        far = 1 if (kind + j) % 2 == 0 else -1
        dz, dy = {
            Y: (0, 1), BACK: (-far, 0), FRONT: (far, 0), FAR: (2, 0),
            BACK_Y: (-far, 1), FRONT_Y: (far, 1), FAR_Y: (2, 1),
        }[name]
        ref = piece(kind, j, dz, dy)
        slot = (j * 2 + kind) * 7 + name
        remote(ref, ref, g_send.at[slot], g_recv.at[slot], y_dev).wait_recv()

    def ahead(kind, j):
        plus = (kind + j) % 2 == 0
        return (up, down, 1) if plus else (down, up, -1)

    def stage0(j):
        for kind in range(2):
            front, back, far = ahead(kind, j)
            if kind == 0:
                own_w[j].wait()
            else:
                pair_w[j].wait_recv()
            send(kind, j, 0, 0, BACK, front)
            send(kind, j, 0, 0, FRONT, back)
            send(kind, j, 0, 0, Y, y_dev)

    def stage1(j):
        front, back, far = ahead(0, j)
        arrived(0, j, Y)
        send(0, j, 0, 1, BACK_Y, front)
        send(0, j, 0, 1, FRONT_Y, back)
        arrived(0, j, BACK)
        send(0, j, -far, 0, FAR, front)
        front, back, far = ahead(1, j)
        arrived(1, j, BACK)
        send(1, j, -far, 0, FAR, front)
        send(1, j, -far, 0, BACK_Y, y_dev)
        arrived(1, j, FRONT)
        send(1, j, far, 0, FRONT_Y, y_dev)

    def stage2(j):
        front, back, far = ahead(0, j)
        arrived(0, j, BACK_Y)
        send(0, j, -far, 1, FAR_Y, front)
        arrived(1, j, FAR)
        send(1, j, 2, 0, FAR_Y, y_dev)

    def near(j):
        arrived(0, j, FRONT)
        arrived(1, j, Y)

    def rest(j):
        for name in (FRONT_Y, FAR, FAR_Y):
            arrived(0, j, name)
        for name in (BACK_Y, FRONT_Y, FAR_Y):
            arrived(1, j, name)

    def contract(js, late):
        places = ((1, 1), (-1, 1), (2, 0), (2, 1)) if late else ((0, 0), (0, 1), (1, 0), (-1, 0))
        starts = [block(dz, dy) * CHIP for dz, dy in places]
        labels = [start + k for start in starts for k in range(CHIP)]

        def one(i, carry):
            left = jnp.concatenate([tv[i, k] for k in labels], axis=1)
            right = []
            for j in js:
                right.append(
                    jnp.concatenate(
                        [
                            wv[j, k] * jnp.full((TILE, TILE), ms[i // HALF, lax.rem(i, HALF) * 8 + j, k], jnp.float32).astype(jnp.bfloat16)
                            for k in labels
                        ],
                        axis=0,
                    )
                )
            right = right[0] if len(js) == 1 else jnp.concatenate(right, axis=1)
            out = jnp.dot(left, right, preferred_element_type=jnp.float32)
            for n, j in enumerate(js):
                tile = out[:, n * TILE : (n + 1) * TILE]
                if late:
                    tile = tile + cyc[j, i]
                    packed, scale = coded(tile.T)
                    code[j, i // HALF, pl.ds(pl.multiple_of(lax.rem(i, HALF) * TILE, TILE), TILE)] = packed
                    carry = carry[:n] + (jnp.where(rows == i + (i // HALF) * 3, scale, carry[n]),) + carry[n + 1 :]
                cyc[j, i] = tile
            return carry

        rows = lax.broadcasted_iota(jnp.int32, (16, TILE), 0)
        scales = lax.fori_loop(0, CHIP, one, tuple(jnp.zeros((16, TILE), jnp.float32) for _ in js))
        if late:
            for n, j in enumerate(js):
                for half in range(2):
                    part = scales[n][half * 8 : half * 8 + 8]
                    code[j, half, HALF * TILE : PACK] = jnp.concatenate([part, part], axis=0).astype(jnp.bfloat16)

    def mirror_half(j, half):
        return mirror.at[j, half]

    def to_y(j):
        return remote(code.at[j, 0], via_y.at[j], y_send.at[j], y_recv.at[j], swapped)

    def to_corner(j):
        slot = lax.rem(delta + 3, 4)
        return remote(code.at[j, 1], via_z.at[slot, j], z_send.at[j], z_recv.at[slot, j], corner)

    def straight(j, half, device):
        send_sem, recv_sem = (a_send, a_recv) if half == 0 else (b_send, b_recv)
        return remote(code.at[j, half], mirror_half(j, half), send_sem.at[j], recv_sem.at[j], device)

    def local(j, half):
        send_sem = a_send if half == 0 else b_send
        return pltpu.make_async_copy(code.at[j, half], mirror_half(j, half), send_sem.at[j])

    def second_a(j):
        return remote(via_y.at[j], mirror_half(j, 0), a_send.at[j], a_recv.at[j], flipped)

    def second_b(j, step):
        device = at(lax.rem(x + step, 4), y_hi, y, z)
        return remote(via_z.at[step - 1, j], mirror_half(j, 1), c_send.at[step - 1, j], b_recv.at[j], device)

    both = jnp.logical_and(crossing, turned)
    only_cross = jnp.logical_and(crossing, diagonal)
    only_turn = jnp.logical_and(jnp.logical_not(crossing), turned)

    def mirror_send(j):
        @pl.when(both)
        def _():
            to_y(j).start()

        @pl.when(only_turn)
        def _():
            straight(j, 0, flipped).start()

        @pl.when(turned)
        def _():
            to_corner(j).start()

        @pl.when(only_cross)
        def _():
            straight(j, 0, swapped).start()
            straight(j, 1, swapped).start()

        @pl.when(stays)
        def _():
            local(j, 0).start()
            local(j, 1).start()

    def mirror_relay(j):
        @pl.when(both)
        def _():
            to_y(j).wait_recv()
            second_a(j).start()

        @pl.when(diagonal)
        def _():
            for step in range(1, 4):
                remote(code.at[j, 1], via_z.at[step - 1, j], z_send.at[j], z_recv.at[step - 1, j], opposite).wait_recv()
                second_b(j, step).start()

    def mirror_wait(j):
        @pl.when(both)
        def _():
            to_y(j).wait_send()
            second_a(j).wait()

        @pl.when(only_turn)
        def _():
            straight(j, 0, flipped).wait()

        @pl.when(turned)
        def _():
            to_corner(j).wait_send()
            straight(j, 1, flipped).wait_recv()

        @pl.when(only_cross)
        def _():
            straight(j, 0, swapped).wait()
            straight(j, 1, swapped).wait()

        @pl.when(stays)
        def _():
            local(j, 0).wait()
            local(j, 1).wait()

        @pl.when(diagonal)
        def _():
            for step in range(1, 4):
                second_b(j, step).wait_send()

    finals = []

    def hand_out(j):
        own = pltpu.make_async_copy(cyc.at[j, pl.ds(c * HALF, HALF)], direct.at[:, c * HALF + j], d_own.at[j])
        own.start()
        pair = remote(
            cyc.at[j, pl.ds(other * HALF, HALF)], direct.at[:, c * HALF + j], d_send.at[j], d_recv.at[j], sibling
        )
        pair.start()

        mirror_send(j)
        finals.append((own, pair))

    t_local = [pltpu.make_async_copy(amp.at[i], tv.at[c * HALF + i], t_own.at[i]) for i in range(HALF)]
    t_pair = [remote(amp.at[i], tv.at[c * HALF + i], t_send.at[i], t_recv.at[i], sibling) for i in range(HALF)]

    stage0(0)
    for i in range(HALF):
        t_local[i].start()
        t_pair[i].start()
    stage0(1)
    make_mask()
    mask_pair.start()
    mask_own.start()
    stage1(0)
    stage0(2)
    stage1(1)
    stage2(0)
    stage0(3)
    stage1(2)
    stage2(1)
    near(0)
    near(1)
    mask_pair.wait()
    mask_own.wait()
    second = pltpu.make_async_copy(mv, ms.at[other], m_sem.at[2])
    second.start()
    second.wait()
    for i in range(HALF):
        t_local[i].wait()
        t_pair[i].wait()
    contract(GROUPS[0], False)
    stage0(4)
    stage1(3)
    stage2(2)
    rest(0)
    rest(1)
    contract(GROUPS[0], True)
    hand_out(0)
    hand_out(1)
    stage1(4)
    stage2(3)
    near(2)
    near(3)
    contract(GROUPS[1], False)
    mirror_relay(0)
    mirror_relay(1)
    stage2(4)
    rest(2)
    rest(3)
    contract(GROUPS[1], True)
    hand_out(2)
    hand_out(3)
    near(4)
    contract(GROUPS[2], False)
    mirror_relay(2)
    mirror_relay(3)
    rest(4)
    contract(GROUPS[2], True)
    hand_out(4)
    mirror_relay(4)

    for copy in sends:
        copy.wait_send()
    for copy in pair_w:
        copy.wait_send()
    for own, pair in finals:
        own.wait()
        pair.wait()
    for j in range(HALF):
        mirror_wait(j)


def coded(tile):
    largest = jnp.max(jnp.max(jnp.abs(tile), axis=0, keepdims=True), axis=1, keepdims=True)
    scale = jnp.broadcast_to(jnp.maximum(largest, 2.0**-100), (16, TILE)).astype(jnp.bfloat16).astype(jnp.float32)
    value = tile * (TOP / scale[:1])
    square = value * value
    fourth = square * square
    eighth = fourth * fourth
    return jnp.where(value < 0, -eighth, eighth).astype(jnp.bfloat16), scale


def finish(direct, mirror, out):
    for half in range(2):
        scales = mirror[0, half, HALF * TILE : PACK].astype(jnp.float32) * (1 / TOP)
        for n in range(HALF):
            value = mirror[0, half, n * TILE : (n + 1) * TILE].astype(jnp.float32)
            root = jnp.sqrt(jnp.sqrt(jnp.sqrt(jnp.abs(value)))) * scales[n : n + 1]
            out[0, half * HALF + n] = direct[0, half * HALF + n] + jnp.where(value < 0, -root, root)


def on_device(amplitudes, integrals, pair_lists, pair_counts):
    bf, f32 = jnp.bfloat16, jnp.float32
    dma = pltpu.SemaphoreType.DMA
    tiles = jax.ShapeDtypeStruct((HALF, CHIP, TILE, TILE), f32)
    anywhere = pl.BlockSpec(memory_space=pl.ANY)
    direct, mirror = pl.pallas_call(
        kernel,
        out_shape=(tiles, jax.ShapeDtypeStruct((HALF, 2, PACK, TILE), bf)),
        in_specs=[anywhere] * 2 + [pl.BlockSpec(memory_space=pltpu.VMEM)] * 2,
        out_specs=(anywhere, anywhere),
        scratch_shapes=[
            pltpu.VMEM((CHIP, O, TILE, TILE), bf),
            pltpu.VMEM((HALF, O, TILE, TILE), bf),
            pltpu.VMEM((HALF, CHIP, TILE, TILE), f32),
            pltpu.VMEM((HALF, 2, PACK, TILE), bf),
            pltpu.VMEM((HALF, PACK, TILE), bf),
            pltpu.VMEM((3, HALF, PACK, TILE), bf),
            pltpu.VMEM((2, 40, TILE), f32),
            pltpu.VMEM((40, TILE), f32),
            pltpu.SMEM((2, 40, TILE), f32),
            dma((HALF,)), dma((HALF,)), dma((HALF,)), dma((HALF,)), dma((HALF,)), dma((HALF,)), dma((3,)),
            dma((70,)), dma((70,)), dma((HALF,)), dma((HALF,)), dma((HALF,)),
            dma((HALF,)), dma((HALF,)), dma((HALF,)), dma((3, HALF)), dma((HALF,)), dma((HALF,)), dma((HALF,)), dma((HALF,)), dma((3, HALF)),
        ],
        compiler_params=pltpu.CompilerParams(
            collective_id=0, has_side_effects=True, vmem_limit_bytes=60 * 1024 * 1024
        ),
        cost_estimate=pl.CostEstimate(flops=17_000_000_000, bytes_accessed=60_000_000, transcendentals=0),
    )(amplitudes, integrals, pair_lists, pair_counts)
    ten = pl.BlockSpec((1, CHIP, TILE, TILE), lambda i: (i, 0, 0, 0))
    return pl.pallas_call(
        finish,
        grid=(HALF,),
        out_shape=tiles,
        in_specs=[ten, pl.BlockSpec((1, 2, PACK, TILE), lambda i: (i, 0, 0, 0))],
        out_specs=ten,
        compiler_params=pltpu.CompilerParams(vmem_limit_bytes=60 * 1024 * 1024),
    )(direct, mirror)


def solution(mesh):
    placed = (
        P("row", None, None, None),
        P("row", "col", None, None),
        P("row", "col", None),
        P("row", "col"),
    )
    return jax.shard_map(
        on_device,
        mesh=mesh,
        in_specs=placed,
        out_specs=P("row", "col", None, None),
        check_vma=False,
    )
```

```python
import functools

import jax
import jax.numpy as jnp
from jax import lax
from jax.experimental import pallas as pl
from jax.experimental.pallas import tpu as pltpu
from jax.sharding import PartitionSpec as P

MESH = pl.DeviceIdType.MESH
TILE = 128
O = 80
HALF = 5
CHIP = 10
Y_FIRST = ((1, 1, 1, 1, 1), (0, 0, 0, 0, 0))
PACK = HALF * TILE + 32
LEG = PACK // 2
SIGNS = (1, -1)
TOP = 2.0**15
Y, BACK, FRONT, FAR, BACK_Y, FRONT_Y, FAR_Y = range(7)


def kernel(
    amp, integ, lists, counts, direct, mirror,
    tv, wv, cyc, code, via_y, via_z, via_s, via_e, mine_v, mv, ms,
    own_sem, pair_send, pair_recv, t_own, t_send, t_recv, m_sem,
    g_send, g_recv, d_own, d_send, d_recv,
    y_send, y_recv, z_send, z_recv, a_send, a_recv, b_send, b_recv, c_send,
    s_send, s_recv, sa_send, sa_recv, e_send, e_recv, e1_send, eb_recv,
):
    row, col = lax.axis_index("row"), lax.axis_index("col")
    z, y, c = row // 4, (row // 2) % 2, row % 2
    chip = row // 2
    other = 1 - c
    sibling = (row + 1 - 2 * c, col)
    y_dev = (row + 2 - 4 * y, col)
    up = (lax.rem(row + 4, 16), col)
    down = (lax.rem(row + 12, 16), col)
    x, y_hi = col // 2, col % 2
    delta = lax.rem(z - x + 4, 4)

    def at(px, lo, hi, pz):
        return (pz * 4 + lo * 2 + c, px * 2 + hi)

    crossing = y != y_hi
    diagonal = delta == 0
    turned = lax.rem(delta, 2) == 1
    across = delta == 2
    sign = jnp.where(delta == 3, 1, -1)
    side = jnp.where(delta == 3, 0, 1)
    stays = jnp.logical_and(diagonal, jnp.logical_not(crossing))
    swapped = at(x, y_hi, y, z)
    flipped = at(z, y, y_hi, x)
    corner = at(x, y, y_hi, x)

    def block(dz, dy):
        return lax.rem(z + dz + 4, 4) * 2 + (y if dy == 0 else 1 - y)

    def near_x(step):
        return at(lax.rem(x + step + 4, 4), y, y_hi, z)

    def aslant(step, cross):
        lo, hi = (y_hi, y) if cross else (y, y_hi)
        return at(lax.rem(x + step + 4, 4), lo, hi, lax.rem(z + step + 4, 4))

    barrier = pltpu.get_barrier_semaphore()

    def greet(device):
        pl.semaphore_signal(barrier, inc=1, device_id=device, device_id_type=MESH)

    for device in (sibling, y_dev, up, down):
        greet(device)

    @pl.when(crossing)
    def _():
        greet(swapped)

    @pl.when(turned)
    def _():
        greet(flipped)
        greet(at(z, y_hi, y, z))
        greet(near_x(sign))
        greet(aslant(sign, True))
        greet(aslant(-sign, True))

    @pl.when(across)
    def _():
        for step in SIGNS:
            greet(near_x(step))
            greet(aslant(step, False))

    @pl.when(jnp.logical_and(across, crossing))
    def _():
        for step in SIGNS:
            greet(aslant(step, True))

    @pl.when(diagonal)
    def _():
        for step in (1, 3):
            greet(at(lax.rem(x + step, 4), y_hi, y, z))

    peers = (
        4 + jnp.where(crossing, 1, 0) + jnp.where(turned, 5, jnp.where(across, jnp.where(crossing, 6, 4), 2))
    )
    pl.semaphore_wait(barrier, peers)

    def remote(src, dst, send, recv, device):
        return pltpu.make_async_remote_copy(
            src_ref=src, dst_ref=dst, send_sem=send, recv_sem=recv, device_id=device, device_id_type=MESH
        )

    mine = pl.ds(chip * CHIP + c * HALF, HALF)
    theirs = pl.ds(chip * CHIP + other * HALF, HALF)
    own_w = [pltpu.make_async_copy(integ.at[:, c * HALF + j], wv.at[j, mine], own_sem.at[j]) for j in range(HALF)]
    pair_w = [
        remote(integ.at[:, other * HALF + j], wv.at[j, mine], pair_send.at[j], pair_recv.at[j], sibling)
        for j in range(HALF)
    ]
    for j in range(HALF):
        own_w[j].start()
        pair_w[j].start()

    mask_pair = remote(mine_v.at[other], mv, m_sem.at[0], m_sem.at[1], sibling)
    mask_own = pltpu.make_async_copy(mine_v.at[c], ms.at[c], m_sem.at[2])

    def make_mask():
        count_rows = counts[...]
        slots = lists.shape[2]
        eye = lax.broadcasted_iota(jnp.int32, (CHIP, CHIP), 0) == lax.broadcasted_iota(jnp.int32, (CHIP, CHIP), 1)
        slot_ids = lax.broadcasted_iota(jnp.int32, (CHIP, slots), 1)
        labels = lax.broadcasted_iota(jnp.int32, (CHIP, TILE), 1)
        for i in range(HALF):
            per_pair = jnp.broadcast_to(count_rows[i : i + 1], (CHIP, CHIP))
            count = jnp.sum(jnp.where(eye, per_pair, 0), axis=1, keepdims=True)
            kept = jnp.where(slot_ids < count, lists[i], -1)
            live = jnp.zeros((CHIP, TILE), jnp.float32)
            for s in range(slots):
                live = jnp.where(kept[:, s : s + 1] == labels, 1.0, live)
            for half in range(2):
                mine_v[half, i * 8 : i * 8 + HALF] = live[half * HALF : (half + 1) * HALF]

    def piece(part, j, dz, dy):
        view = pl.ds(block(dz, dy) * CHIP + (c if part == 0 else other) * HALF, HALF)
        return wv.at[j, view]

    sends = []

    def send(part, j, dz, dy, name, device):
        ref = piece(part, j, dz, dy)
        slot = (j * 2 + part) * 7 + name
        copy = remote(ref, ref, g_send.at[slot], g_recv.at[slot], device)
        copy.start()
        sends.append(copy)

    def arrived(part, j, name):
        far = ahead(part, j)[2]
        dz, dy = {
            Y: (0, 1), BACK: (-far, 0), FRONT: (far, 0), FAR: (2, 0),
            BACK_Y: (-far, 1), FRONT_Y: (far, 1), FAR_Y: (2, 1),
        }[name]
        ref = piece(part, j, dz, dy)
        slot = (j * 2 + part) * 7 + name
        remote(ref, ref, g_send.at[slot], g_recv.at[slot], y_dev).wait_recv()

    def ahead(part, j):
        return (up, down, 1) if (part + j) % 2 == 0 else (down, up, -1)

    def own(part, j):
        front, back, far = ahead(part, j)
        if part == 0:
            own_w[j].wait()
        else:
            pair_w[j].wait_recv()
        send(part, j, 0, 0, BACK, front)
        send(part, j, 0, 0, FRONT, back)
        send(part, j, 0, 0, Y, y_dev)

    def first(part, j):
        front, back, far = ahead(part, j)
        if Y_FIRST[part][j]:
            arrived(part, j, Y)
            send(part, j, 0, 1, BACK_Y, front)
            send(part, j, 0, 1, FRONT_Y, back)
            arrived(part, j, BACK)
            send(part, j, -far, 0, FAR, front)
        else:
            arrived(part, j, BACK)
            send(part, j, -far, 0, FAR, front)
            send(part, j, -far, 0, BACK_Y, y_dev)
            arrived(part, j, FRONT)
            send(part, j, far, 0, FRONT_Y, y_dev)

    def second(part, j):
        front, back, far = ahead(part, j)
        if Y_FIRST[part][j]:
            arrived(part, j, BACK_Y)
            send(part, j, -far, 1, FAR_Y, front)
        else:
            arrived(part, j, FAR)
            send(part, j, 2, 0, FAR_Y, y_dev)

    def near(j):
        for part in range(2):
            arrived(part, j, FRONT if Y_FIRST[part][j] else Y)

    def rest(j):
        for part in range(2):
            for name in (FRONT_Y, FAR, FAR_Y) if Y_FIRST[part][j] else (BACK_Y, FRONT_Y, FAR_Y):
                arrived(part, j, name)

    def stage0(j):
        own(0, j)
        own(1, j)

    def stage1(j):
        first(0, j)
        first(1, j)

    def stage2(j):
        second(0, j)
        second(1, j)

    def contract(js, late):
        places = ((1, 1), (-1, 1), (2, 0), (2, 1)) if late else ((0, 0), (0, 1), (1, 0), (-1, 0))
        starts = [block(dz, dy) * CHIP for dz, dy in places]
        labels = [start + k for start in starts for k in range(CHIP)]

        def one(i, carry):
            left = jnp.concatenate([tv[i, k] for k in labels], axis=1)
            right = []
            for j in js:
                right.append(
                    jnp.concatenate(
                        [
                            wv[j, k] * jnp.full((TILE, TILE), ms[i // HALF, lax.rem(i, HALF) * 8 + j, k], jnp.float32).astype(jnp.bfloat16)
                            for k in labels
                        ],
                        axis=0,
                    )
                )
            right = right[0] if len(js) == 1 else jnp.concatenate(right, axis=1)
            out = jnp.dot(left, right, preferred_element_type=jnp.float32)
            for n, j in enumerate(js):
                tile = out[:, n * TILE : (n + 1) * TILE]
                if late:
                    tile = tile + cyc[j, i]
                    packed, scale = coded(tile.T)
                    code[j, i // HALF, pl.ds(pl.multiple_of(lax.rem(i, HALF) * TILE, TILE), TILE)] = packed
                    carry = carry[:n] + (jnp.where(rows == i + (i // HALF) * 3, scale, carry[n]),) + carry[n + 1 :]
                cyc[j, i] = tile
            return carry

        rows = lax.broadcasted_iota(jnp.int32, (16, TILE), 0)
        scales = lax.fori_loop(0, CHIP, one, tuple(jnp.zeros((16, TILE), jnp.float32) for _ in js))
        if late:
            for n, j in enumerate(js):
                for half in range(2):
                    part = scales[n][half * 8 : half * 8 + 8]
                    code[j, half, HALF * TILE : PACK] = jnp.concatenate([part] * 4, axis=0).astype(jnp.bfloat16)

    def mirror_half(j, half):
        return mirror.at[j, half]

    def to_y(j):
        return remote(code.at[j, 0], via_y.at[j], y_send.at[j], y_recv.at[j], swapped)

    def to_corner(j):
        slot = lax.rem(delta + 3, 4)
        return remote(code.at[j, 1], via_z.at[slot, j], z_send.at[j], z_recv.at[slot, j], corner)

    def straight(j, half, device):
        send_sem, recv_sem = (a_send, a_recv) if half == 0 else (b_send, b_recv)
        return remote(code.at[j, half], mirror_half(j, half), send_sem.at[j], recv_sem.at[j], device)

    def local(j, half):
        send_sem = a_send if half == 0 else b_send
        return pltpu.make_async_copy(code.at[j, half], mirror_half(j, half), send_sem.at[j])

    def second_a(j):
        return remote(via_y.at[j], mirror_half(j, 0), a_send.at[j], a_recv.at[j], flipped)

    def second_b(j, step):
        device = at(lax.rem(x + step, 4), y_hi, y, z)
        return remote(via_z.at[step - 1, j], mirror_half(j, 1), c_send.at[step - 1, j], b_recv.at[j], device)

    def leg(d):
        return pl.ds(d * LEG, LEG)

    def slant_out(j, d):
        return remote(
            code.at[j, 0, leg(d)], via_s.at[d, j], s_send.at[d, j], s_recv.at[d, j], aslant(SIGNS[d], True)
        )

    def slant_in(j, d):
        return remote(
            via_s.at[d, j], mirror.at[j, 0, leg(d)], sa_send.at[d, j], sa_recv.at[d, j], aslant(SIGNS[d], False)
        )

    def edge_out(j, d):
        return remote(
            code.at[j, 1, leg(d)], via_e.at[0, j], e_send.at[d, j], e_recv.at[0, j], up if d == 0 else down
        )

    def edge_mid(j):
        return remote(via_e.at[0, j], via_e.at[1, j], e1_send.at[0, j], e_recv.at[1, j], aslant(sign, True))

    def edge_in(j):
        rows = pl.ds(pl.multiple_of(side * LEG, 16), LEG)
        return remote(via_e.at[1, j], mirror.at[j, 1, rows], e1_send.at[1, j], eb_recv.at[side, j], near_x(sign))

    both = jnp.logical_and(crossing, turned)
    only_cross = jnp.logical_and(crossing, diagonal)
    only_turn = jnp.logical_and(jnp.logical_not(crossing), turned)

    def mirror_send(j):
        @pl.when(both)
        def _():
            to_y(j).start()

        @pl.when(only_turn)
        def _():
            straight(j, 0, flipped).start()

        @pl.when(turned)
        def _():
            to_corner(j).start()

        @pl.when(across)
        def _():
            for d in range(2):
                slant_out(j, d).start()
                edge_out(j, d).start()

        @pl.when(only_cross)
        def _():
            straight(j, 0, swapped).start()
            straight(j, 1, swapped).start()

        @pl.when(stays)
        def _():
            local(j, 0).start()
            local(j, 1).start()

    def mirror_relay(j):
        @pl.when(both)
        def _():
            to_y(j).wait_recv()
            second_a(j).start()

        @pl.when(diagonal)
        def _():
            for step in (1, 3):
                remote(code.at[j, 1], via_z.at[step - 1, j], z_send.at[j], z_recv.at[step - 1, j], sibling).wait_recv()
                second_b(j, step).start()

        @pl.when(across)
        def _():
            for d in range(2):
                slant_out(j, d).wait_recv()
                slant_in(j, d).start()

        @pl.when(turned)
        def _():
            edge_out(j, 0).wait_recv()
            edge_mid(j).start()

    def mirror_last(j):
        @pl.when(turned)
        def _():
            edge_mid(j).wait_recv()
            edge_in(j).start()

    def mirror_wait(j):
        @pl.when(across)
        def _():
            for d in range(2):
                slant_out(j, d).wait_send()
                slant_in(j, d).wait()
                edge_out(j, d).wait_send()
                remote(
                    code.at[j, 1, leg(d)], mirror.at[j, 1, leg(d)], e_send.at[d, j], eb_recv.at[d, j], sibling
                ).wait_recv()

        @pl.when(turned)
        def _():
            edge_mid(j).wait_send()
            edge_in(j).wait_send()

        @pl.when(both)
        def _():
            to_y(j).wait_send()
            second_a(j).wait()

        @pl.when(only_turn)
        def _():
            straight(j, 0, flipped).wait()

        @pl.when(turned)
        def _():
            to_corner(j).wait_send()
            straight(j, 1, flipped).wait_recv()

        @pl.when(only_cross)
        def _():
            straight(j, 0, swapped).wait()
            straight(j, 1, swapped).wait()

        @pl.when(stays)
        def _():
            local(j, 0).wait()
            local(j, 1).wait()

        @pl.when(diagonal)
        def _():
            for step in (1, 3):
                second_b(j, step).wait_send()

    finals = []

    def hand_out(j):
        keep = pltpu.make_async_copy(cyc.at[j, pl.ds(c * HALF, HALF)], direct.at[:, c * HALF + j], d_own.at[j])
        keep.start()
        pair = remote(
            cyc.at[j, pl.ds(other * HALF, HALF)], direct.at[:, c * HALF + j], d_send.at[j], d_recv.at[j], sibling
        )
        pair.start()

        mirror_send(j)
        finals.append((keep, pair))

    t_local = [pltpu.make_async_copy(amp.at[i], tv.at[c * HALF + i], t_own.at[i]) for i in range(HALF)]
    t_pair = [remote(amp.at[i], tv.at[c * HALF + i], t_send.at[i], t_recv.at[i], sibling) for i in range(HALF)]

    stage0(0)
    for i in range(HALF):
        t_local[i].start()
        t_pair[i].start()
    stage0(1)
    make_mask()
    mask_pair.start()
    mask_own.start()
    stage1(0)
    stage2(0)
    mask_pair.wait()
    mask_own.wait()
    mask_theirs = pltpu.make_async_copy(mv, ms.at[other], m_sem.at[2])
    mask_theirs.start()
    mask_theirs.wait()
    for i in range(HALF):
        t_local[i].wait()
        t_pair[i].wait()
    stage1(1)
    stage0(2)
    near(0)
    contract((0,), False)
    rest(0)
    contract((0,), True)
    hand_out(0)
    stage2(1)
    stage1(2)
    stage0(3)
    near(1)
    contract((1,), False)
    rest(1)
    contract((1,), True)
    hand_out(1)
    mirror_relay(0)
    stage2(2)
    stage1(3)
    stage0(4)
    near(2)
    contract((2,), False)
    rest(2)
    contract((2,), True)
    hand_out(2)
    mirror_relay(1)
    mirror_last(0)
    stage2(3)
    stage1(4)
    near(3)
    contract((3,), False)
    rest(3)
    contract((3,), True)
    hand_out(3)
    mirror_relay(2)
    mirror_last(1)
    stage2(4)
    near(4)
    contract((4,), False)
    mirror_relay(3)
    mirror_last(2)
    rest(4)
    contract((4,), True)
    hand_out(4)
    mirror_relay(4)
    mirror_last(3)
    mirror_last(4)

    for copy in sends:
        copy.wait_send()
    for copy in pair_w:
        copy.wait_send()
    for keep, pair in finals:
        keep.wait()
        pair.wait()
    for j in range(HALF):
        mirror_wait(j)


def coded(tile):
    largest = jnp.max(jnp.max(jnp.abs(tile), axis=0, keepdims=True), axis=1, keepdims=True)
    scale = jnp.broadcast_to(jnp.maximum(largest, 2.0**-100), (16, TILE)).astype(jnp.bfloat16).astype(jnp.float32)
    value = tile * (TOP / scale[:1])
    square = value * value
    fourth = square * square
    eighth = fourth * fourth
    return jnp.where(value < 0, -eighth, eighth).astype(jnp.bfloat16), scale


def finish(direct, mirror, out):
    for half in range(2):
        scales = mirror[0, half, HALF * TILE : PACK].astype(jnp.float32) * (1 / TOP)
        for n in range(HALF):
            value = mirror[0, half, n * TILE : (n + 1) * TILE].astype(jnp.float32)
            root = jnp.sqrt(jnp.sqrt(jnp.sqrt(jnp.abs(value)))) * scales[n : n + 1]
            out[0, half * HALF + n] = direct[0, half * HALF + n] + jnp.where(value < 0, -root, root)


def on_device(amplitudes, integrals, pair_lists, pair_counts):
    bf, f32 = jnp.bfloat16, jnp.float32
    dma = pltpu.SemaphoreType.DMA
    tiles = jax.ShapeDtypeStruct((HALF, CHIP, TILE, TILE), f32)
    anywhere = pl.BlockSpec(memory_space=pl.ANY)
    direct, mirror = pl.pallas_call(
        kernel,
        out_shape=(tiles, jax.ShapeDtypeStruct((HALF, 2, PACK, TILE), bf)),
        in_specs=[anywhere] * 2 + [pl.BlockSpec(memory_space=pltpu.VMEM)] * 2,
        out_specs=(anywhere, anywhere),
        scratch_shapes=[
            pltpu.VMEM((CHIP, O, TILE, TILE), bf),
            pltpu.VMEM((HALF, O, TILE, TILE), bf),
            pltpu.VMEM((HALF, CHIP, TILE, TILE), f32),
            pltpu.VMEM((HALF, 2, PACK, TILE), bf),
            pltpu.VMEM((HALF, PACK, TILE), bf),
            pltpu.VMEM((3, HALF, PACK, TILE), bf),
            pltpu.VMEM((2, HALF, LEG, TILE), bf),
            pltpu.VMEM((2, HALF, LEG, TILE), bf),
            pltpu.VMEM((2, 40, TILE), f32),
            pltpu.VMEM((40, TILE), f32),
            pltpu.SMEM((2, 40, TILE), f32),
            dma((HALF,)), dma((HALF,)), dma((HALF,)), dma((HALF,)), dma((HALF,)), dma((HALF,)), dma((3,)),
            dma((70,)), dma((70,)), dma((HALF,)), dma((HALF,)), dma((HALF,)),
            dma((HALF,)), dma((HALF,)), dma((HALF,)), dma((3, HALF)), dma((HALF,)), dma((HALF,)), dma((HALF,)), dma((HALF,)), dma((3, HALF)),
            dma((2, HALF)), dma((2, HALF)), dma((2, HALF)), dma((2, HALF)), dma((2, HALF)), dma((2, HALF)), dma((2, HALF)), dma((2, HALF)),
        ],
        compiler_params=pltpu.CompilerParams(
            collective_id=0, has_side_effects=True, vmem_limit_bytes=60 * 1024 * 1024
        ),
        cost_estimate=pl.CostEstimate(flops=17_000_000_000, bytes_accessed=60_000_000, transcendentals=0),
    )(amplitudes, integrals, pair_lists, pair_counts)
    ten = pl.BlockSpec((1, CHIP, TILE, TILE), lambda i: (i, 0, 0, 0))
    return pl.pallas_call(
        finish,
        grid=(HALF,),
        out_shape=tiles,
        in_specs=[ten, pl.BlockSpec((1, 2, PACK, TILE), lambda i: (i, 0, 0, 0))],
        out_specs=ten,
        compiler_params=pltpu.CompilerParams(vmem_limit_bytes=60 * 1024 * 1024),
    )(direct, mirror)


def solution(mesh):
    placed = (
        P("row", None, None, None),
        P("row", "col", None, None),
        P("row", "col", None),
        P("row", "col"),
    )
    return jax.shard_map(
        on_device,
        mesh=mesh,
        in_specs=placed,
        out_specs=P("row", "col", None, None),
        check_vma=False,
    )
```

```python
import functools

import jax
import jax.numpy as jnp
from jax import lax
from jax.experimental import pallas as pl
from jax.experimental.pallas import tpu as pltpu
from jax.sharding import PartitionSpec as P

MESH = pl.DeviceIdType.MESH
TILE = 128
O = 80
HALF = 5
CHIP = 10
Y_FIRST = ((1, 1, 1, 1, 1), (0, 0, 0, 0, 0))
PACK = HALF * TILE + 32
LEG = PACK // 2
SIGNS = (1, -1)
TOP = 2.0**15
Y, BACK, FRONT, FAR, BACK_Y, FRONT_Y, FAR_Y = range(7)


def kernel(
    amp, integ, lists, counts, direct, mirror,
    tv, wv, cyc, code, via_y, via_z, via_s, via_e, mine_v, mv, ms,
    own_sem, pair_send, pair_recv, t_own, t_send, t_recv, m_sem,
    g_send, g_recv, d_own, d_send, d_recv,
    y_send, y_recv, z_send, z_recv, a_send, a_recv, b_send, b_recv, c_send,
    s_send, s_recv, sa_send, sa_recv, e_send, e_recv, e1_send, eb_recv,
):
    row, col = lax.axis_index("row"), lax.axis_index("col")
    z, y, c = row // 4, (row // 2) % 2, row % 2
    chip = row // 2
    other = 1 - c
    sibling = (row + 1 - 2 * c, col)
    y_dev = (row + 2 - 4 * y, col)
    up = (lax.rem(row + 4, 16), col)
    down = (lax.rem(row + 12, 16), col)
    x, y_hi = col // 2, col % 2
    delta = lax.rem(z - x + 4, 4)

    def at(px, lo, hi, pz):
        return (pz * 4 + lo * 2 + c, px * 2 + hi)

    crossing = y != y_hi
    diagonal = delta == 0
    turned = lax.rem(delta, 2) == 1
    across = delta == 2
    sign = jnp.where(delta == 3, 1, -1)
    side = jnp.where(delta == 3, 0, 1)
    stays = jnp.logical_and(diagonal, jnp.logical_not(crossing))
    swapped = at(x, y_hi, y, z)
    flipped = at(z, y, y_hi, x)
    corner = at(x, y, y_hi, x)

    def block(dz, dy):
        return lax.rem(z + dz + 4, 4) * 2 + (y if dy == 0 else 1 - y)

    def near_x(step):
        return at(lax.rem(x + step + 4, 4), y, y_hi, z)

    def aslant(step, cross):
        lo, hi = (y_hi, y) if cross else (y, y_hi)
        return at(lax.rem(x + step + 4, 4), lo, hi, lax.rem(z + step + 4, 4))

    barrier = pltpu.get_barrier_semaphore()

    def greet(device):
        pl.semaphore_signal(barrier, inc=1, device_id=device, device_id_type=MESH)

    for device in (sibling, y_dev, up, down):
        greet(device)

    @pl.when(crossing)
    def _():
        greet(swapped)

    @pl.when(turned)
    def _():
        greet(flipped)
        greet(at(z, y_hi, y, z))
        greet(near_x(sign))
        greet(aslant(sign, True))
        greet(aslant(-sign, True))

    @pl.when(across)
    def _():
        for step in SIGNS:
            greet(near_x(step))
            greet(aslant(step, False))

    @pl.when(jnp.logical_and(across, crossing))
    def _():
        for step in SIGNS:
            greet(aslant(step, True))

    @pl.when(diagonal)
    def _():
        for step in (1, 3):
            greet(at(lax.rem(x + step, 4), y_hi, y, z))

    peers = (
        4 + jnp.where(crossing, 1, 0) + jnp.where(turned, 5, jnp.where(across, jnp.where(crossing, 6, 4), 2))
    )
    pl.semaphore_wait(barrier, peers)

    def remote(src, dst, send, recv, device):
        return pltpu.make_async_remote_copy(
            src_ref=src, dst_ref=dst, send_sem=send, recv_sem=recv, device_id=device, device_id_type=MESH
        )

    mine = pl.ds(chip * CHIP + c * HALF, HALF)
    theirs = pl.ds(chip * CHIP + other * HALF, HALF)
    own_w = [pltpu.make_async_copy(integ.at[:, c * HALF + j], wv.at[j, mine], own_sem.at[j]) for j in range(HALF)]
    pair_w = [
        remote(integ.at[:, other * HALF + j], wv.at[j, mine], pair_send.at[j], pair_recv.at[j], sibling)
        for j in range(HALF)
    ]
    for j in range(HALF):
        own_w[j].start()
        pair_w[j].start()

    mask_pair = remote(mine_v.at[other], mv, m_sem.at[0], m_sem.at[1], sibling)
    mask_own = pltpu.make_async_copy(mine_v.at[c], ms.at[c], m_sem.at[2])

    def make_mask():
        count_rows = counts[...]
        slots = lists.shape[2]
        eye = lax.broadcasted_iota(jnp.int32, (CHIP, CHIP), 0) == lax.broadcasted_iota(jnp.int32, (CHIP, CHIP), 1)
        slot_ids = lax.broadcasted_iota(jnp.int32, (CHIP, slots), 1)
        labels = lax.broadcasted_iota(jnp.int32, (CHIP, TILE), 1)
        for i in range(HALF):
            per_pair = jnp.broadcast_to(count_rows[i : i + 1], (CHIP, CHIP))
            count = jnp.sum(jnp.where(eye, per_pair, 0), axis=1, keepdims=True)
            kept = jnp.where(slot_ids < count, lists[i], -1)
            live = jnp.zeros((CHIP, TILE), jnp.float32)
            for s in range(slots):
                live = jnp.where(kept[:, s : s + 1] == labels, 1.0, live)
            for half in range(2):
                mine_v[half, i * 8 : i * 8 + HALF] = live[half * HALF : (half + 1) * HALF]

    def piece(part, j, dz, dy):
        view = pl.ds(block(dz, dy) * CHIP + (c if part == 0 else other) * HALF, HALF)
        return wv.at[j, view]

    sends = []

    def send(part, j, dz, dy, name, device):
        ref = piece(part, j, dz, dy)
        slot = (j * 2 + part) * 7 + name
        src = integ.at[:, c * HALF + j] if part == 0 and (dz, dy) == (0, 0) else ref
        remote(src, ref, g_send.at[slot], g_recv.at[slot], device).start()
        sends.append((part, j, dz, dy, name, device))

    def sent(part, j, dz, dy, name, device):
        ref = piece(part, j, dz, dy)
        slot = (j * 2 + part) * 7 + name
        remote(ref, ref, g_send.at[slot], g_recv.at[slot], device).wait_send()

    def arrived(part, j, name):
        far = ahead(part, j)[2]
        dz, dy = {
            Y: (0, 1), BACK: (-far, 0), FRONT: (far, 0), FAR: (2, 0),
            BACK_Y: (-far, 1), FRONT_Y: (far, 1), FAR_Y: (2, 1),
        }[name]
        ref = piece(part, j, dz, dy)
        slot = (j * 2 + part) * 7 + name
        remote(ref, ref, g_send.at[slot], g_recv.at[slot], y_dev).wait_recv()

    def ahead(part, j):
        return (up, down, 1) if (part + j) % 2 == 0 else (down, up, -1)

    def own(part, j):
        front, back, far = ahead(part, j)
        if part == 1:
            pair_w[j].wait_recv()
        send(part, j, 0, 0, BACK, front)
        send(part, j, 0, 0, FRONT, back)
        send(part, j, 0, 0, Y, y_dev)

    def first(part, j):
        front, back, far = ahead(part, j)
        if Y_FIRST[part][j]:
            arrived(part, j, Y)
            send(part, j, 0, 1, BACK_Y, front)
            send(part, j, 0, 1, FRONT_Y, back)
            arrived(part, j, BACK)
            send(part, j, -far, 0, FAR, front)
        else:
            arrived(part, j, BACK)
            send(part, j, -far, 0, FAR, front)
            send(part, j, -far, 0, BACK_Y, y_dev)
            arrived(part, j, FRONT)
            send(part, j, far, 0, FRONT_Y, y_dev)

    def second(part, j):
        front, back, far = ahead(part, j)
        if Y_FIRST[part][j]:
            arrived(part, j, BACK_Y)
            send(part, j, -far, 1, FAR_Y, front)
        else:
            arrived(part, j, FAR)
            send(part, j, 2, 0, FAR_Y, y_dev)

    def near(j):
        own_w[j].wait()
        for part in range(2):
            arrived(part, j, FRONT if Y_FIRST[part][j] else Y)

    def rest(j):
        for part in range(2):
            for name in (FRONT_Y, FAR) if Y_FIRST[part][j] else (BACK_Y, FRONT_Y):
                arrived(part, j, name)

    def last(j):
        for part in range(2):
            arrived(part, j, FAR_Y)

    def stage0(j):
        own(0, j)
        own(1, j)

    def stage1(j):
        first(0, j)
        first(1, j)

    def stage2(j):
        second(0, j)
        second(1, j)

    near_places = ((0, 0), (0, 1), (1, 0), (-1, 0))
    rest_places = ((1, 1), (-1, 1), (2, 0))
    last_places = ((2, 1),)

    def contract(j, places, i_from, i_to, final, hooks):
        starts = [block(dz, dy) * CHIP for dz, dy in places]
        labels = [start + k for start in starts for k in range(CHIP)]
        opening = places[0] == (0, 0)

        def one(i, scales):
            for step, hook in hooks.items():
                pl.when(i == step)(hook)
            left = jnp.concatenate([tv[i, k] for k in labels], axis=1)
            right = jnp.concatenate(
                [
                    wv[j, k]
                    * jnp.full((TILE, TILE), ms[i // HALF, lax.rem(i, HALF) * 8 + j, k], jnp.float32).astype(jnp.bfloat16)
                    for k in labels
                ],
                axis=0,
            )
            tile = jnp.dot(left, right, preferred_element_type=jnp.float32)
            if not opening:
                tile = tile + cyc[j, i]
            if final:
                n = i - i_from
                packed, scale = coded(tile.T)
                code[j, i_from // HALF, pl.ds(pl.multiple_of(n * TILE, TILE), TILE)] = packed
                scales = jnp.where(rows == n, scale[:8], scales)
            cyc[j, i] = tile
            return scales

        rows = lax.broadcasted_iota(jnp.int32, (8, TILE), 0)
        scales = lax.fori_loop(i_from, i_to, one, jnp.zeros((8, TILE), jnp.float32))
        if final:
            code[j, i_from // HALF, HALF * TILE : PACK] = jnp.concatenate([scales] * 4, axis=0).astype(jnp.bfloat16)

    def begin(j, hooks):
        contract(j, near_places, 0, CHIP, False, hooks)

    def carry_on(j, hooks):
        contract(j, rest_places, 0, CHIP, False, hooks)

    def end(j, places, hooks):
        for half in range(2):
            contract(j, places, half * HALF, (half + 1) * HALF, True, hooks)
            mirror_send(j, half)
        hand_out(j)

    def mirror_half(j, half):
        return mirror.at[j, half]

    def to_y(j):
        return remote(code.at[j, 0], via_y.at[j], y_send.at[j], y_recv.at[j], swapped)

    def to_corner(j):
        slot = lax.rem(delta + 3, 4)
        return remote(code.at[j, 1], via_z.at[slot, j], z_send.at[j], z_recv.at[slot, j], corner)

    def straight(j, half, device):
        send_sem, recv_sem = (a_send, a_recv) if half == 0 else (b_send, b_recv)
        return remote(code.at[j, half], mirror_half(j, half), send_sem.at[j], recv_sem.at[j], device)

    def local(j, half):
        send_sem = a_send if half == 0 else b_send
        return pltpu.make_async_copy(code.at[j, half], mirror_half(j, half), send_sem.at[j])

    def second_a(j):
        return remote(via_y.at[j], mirror_half(j, 0), a_send.at[j], a_recv.at[j], flipped)

    def second_b(j, step):
        device = at(lax.rem(x + step, 4), y_hi, y, z)
        return remote(via_z.at[step - 1, j], mirror_half(j, 1), c_send.at[step - 1, j], b_recv.at[j], device)

    def leg(d):
        return pl.ds(d * LEG, LEG)

    def slant_out(j, d):
        return remote(
            code.at[j, 0, leg(d)], via_s.at[d, j], s_send.at[d, j], s_recv.at[d, j], aslant(SIGNS[d], True)
        )

    def slant_in(j, d):
        return remote(
            via_s.at[d, j], mirror.at[j, 0, leg(d)], sa_send.at[d, j], sa_recv.at[d, j], aslant(SIGNS[d], False)
        )

    def edge_out(j, d):
        return remote(
            code.at[j, 1, leg(d)], via_e.at[0, j], e_send.at[d, j], e_recv.at[0, j], up if d == 0 else down
        )

    def edge_mid(j):
        return remote(via_e.at[0, j], via_e.at[1, j], e1_send.at[0, j], e_recv.at[1, j], aslant(sign, True))

    def edge_in(j):
        rows = pl.ds(pl.multiple_of(side * LEG, 16), LEG)
        return remote(via_e.at[1, j], mirror.at[j, 1, rows], e1_send.at[1, j], eb_recv.at[side, j], near_x(sign))

    both = jnp.logical_and(crossing, turned)
    only_cross = jnp.logical_and(crossing, diagonal)
    only_turn = jnp.logical_and(jnp.logical_not(crossing), turned)

    def mirror_send(j, half):
        if half == 0:
            pl.when(both)(lambda: to_y(j).start())
            pl.when(only_turn)(lambda: straight(j, 0, flipped).start())
        else:
            pl.when(turned)(lambda: to_corner(j).start())
        pl.when(only_cross)(lambda: straight(j, half, swapped).start())
        pl.when(stays)(lambda: local(j, half).start())

        @pl.when(across)
        def _():
            for d in range(2):
                (slant_out if half == 0 else edge_out)(j, d).start()

    def mirror_relay(j):
        @pl.when(both)
        def _():
            to_y(j).wait_recv()
            second_a(j).start()

        @pl.when(diagonal)
        def _():
            for step in (1, 3):
                remote(code.at[j, 1], via_z.at[step - 1, j], z_send.at[j], z_recv.at[step - 1, j], sibling).wait_recv()
                second_b(j, step).start()

        @pl.when(across)
        def _():
            for d in range(2):
                slant_out(j, d).wait_recv()
                slant_in(j, d).start()

        @pl.when(turned)
        def _():
            edge_out(j, 0).wait_recv()
            edge_mid(j).start()

    def mirror_last(j):
        @pl.when(turned)
        def _():
            edge_mid(j).wait_recv()
            edge_in(j).start()

    def mirror_wait(j):
        @pl.when(across)
        def _():
            for d in range(2):
                slant_out(j, d).wait_send()
                slant_in(j, d).wait()
                edge_out(j, d).wait_send()
                remote(
                    code.at[j, 1, leg(d)], mirror.at[j, 1, leg(d)], e_send.at[d, j], eb_recv.at[d, j], sibling
                ).wait_recv()

        @pl.when(turned)
        def _():
            edge_mid(j).wait_send()
            edge_in(j).wait_send()

        @pl.when(both)
        def _():
            to_y(j).wait_send()
            second_a(j).wait()

        @pl.when(only_turn)
        def _():
            straight(j, 0, flipped).wait()

        @pl.when(turned)
        def _():
            to_corner(j).wait_send()
            straight(j, 1, flipped).wait_recv()

        @pl.when(only_cross)
        def _():
            straight(j, 0, swapped).wait()
            straight(j, 1, swapped).wait()

        @pl.when(stays)
        def _():
            local(j, 0).wait()
            local(j, 1).wait()

        @pl.when(diagonal)
        def _():
            for step in (1, 3):
                second_b(j, step).wait_send()

    finals = []

    def hand_out(j):
        keep = pltpu.make_async_copy(cyc.at[j, pl.ds(c * HALF, HALF)], direct.at[:, c * HALF + j], d_own.at[j])
        keep.start()
        pair = remote(
            cyc.at[j, pl.ds(other * HALF, HALF)], direct.at[:, c * HALF + j], d_send.at[j], d_recv.at[j], sibling
        )
        pair.start()

        finals.append((keep, pair))

    t_local = [pltpu.make_async_copy(amp.at[i], tv.at[c * HALF + i], t_own.at[i]) for i in range(HALF)]
    t_pair = [remote(amp.at[i], tv.at[c * HALF + i], t_send.at[i], t_recv.at[i], sibling) for i in range(HALF)]

    stage0(0)
    for i in range(HALF):
        t_local[i].start()
        t_pair[i].start()
    stage0(1)
    make_mask()
    mask_pair.start()
    mask_own.start()
    stage1(0)
    stage2(0)
    mask_pair.wait()
    mask_own.wait()
    mask_theirs = pltpu.make_async_copy(mv, ms.at[other], m_sem.at[2])
    mask_theirs.start()
    mask_theirs.wait()
    for i in range(HALF):
        t_local[i].wait()
        t_pair[i].wait()
    stage1(1)
    stage0(2)
    near(0)
    begin(0, {})
    rest(0)
    last(0)
    end(0, rest_places + last_places, {})
    stage2(1)
    stage1(2)
    stage0(3)
    near(1)
    begin(1, {})
    rest(1)
    last(1)
    end(1, rest_places + last_places, {})
    mirror_relay(0)
    stage2(2)
    stage1(3)
    stage0(4)
    near(2)
    begin(2, {})
    rest(2)
    last(2)
    end(2, rest_places + last_places, {})
    mirror_relay(1)
    mirror_last(0)
    stage2(3)
    stage1(4)
    near(3)
    begin(3, {})
    rest(3)
    last(3)
    end(3, rest_places + last_places, {})
    mirror_relay(2)
    mirror_last(1)
    stage2(4)
    near(4)
    begin(4, {})
    mirror_relay(3)
    mirror_last(2)
    rest(4)
    last(4)
    end(4, rest_places + last_places, {})
    mirror_last(3)
    mirror_relay(4)
    mirror_last(4)

    for way in sends:
        sent(*way)
    for copy in pair_w:
        copy.wait_send()
    for keep, pair in finals:
        keep.wait()
        pair.wait()
    for j in range(HALF):
        mirror_wait(j)


def coded(tile):
    largest = jnp.max(jnp.max(jnp.abs(tile), axis=0, keepdims=True), axis=1, keepdims=True)
    scale = jnp.broadcast_to(jnp.maximum(largest, 2.0**-100), (16, TILE)).astype(jnp.bfloat16).astype(jnp.float32)
    value = tile * (TOP / scale[:1])
    square = value * value
    fourth = square * square
    eighth = fourth * fourth
    return jnp.where(value < 0, -eighth, eighth).astype(jnp.bfloat16), scale


def finish(direct, mirror, out):
    for half in range(2):
        scales = mirror[0, half, HALF * TILE : PACK].astype(jnp.float32) * (1 / TOP)
        for n in range(HALF):
            value = mirror[0, half, n * TILE : (n + 1) * TILE].astype(jnp.float32)
            inverse = lax.rsqrt(jnp.maximum(jnp.abs(value), 2.0**-126))
            quarter = lax.rsqrt(inverse)
            root = quarter * lax.rsqrt(quarter) * scales[n : n + 1]
            out[0, half * HALF + n] = direct[0, half * HALF + n] + jnp.where(value < 0, -root, root)


def on_device(amplitudes, integrals, pair_lists, pair_counts):
    bf, f32 = jnp.bfloat16, jnp.float32
    dma = pltpu.SemaphoreType.DMA
    tiles = jax.ShapeDtypeStruct((HALF, CHIP, TILE, TILE), f32)
    anywhere = pl.BlockSpec(memory_space=pl.ANY)
    direct, mirror = pl.pallas_call(
        kernel,
        out_shape=(tiles, jax.ShapeDtypeStruct((HALF, 2, PACK, TILE), bf)),
        in_specs=[anywhere] * 2 + [pl.BlockSpec(memory_space=pltpu.VMEM)] * 2,
        out_specs=(anywhere, anywhere),
        scratch_shapes=[
            pltpu.VMEM((CHIP, O, TILE, TILE), bf),
            pltpu.VMEM((HALF, O, TILE, TILE), bf),
            pltpu.VMEM((HALF, CHIP, TILE, TILE), f32),
            pltpu.VMEM((HALF, 2, PACK, TILE), bf),
            pltpu.VMEM((HALF, PACK, TILE), bf),
            pltpu.VMEM((3, HALF, PACK, TILE), bf),
            pltpu.VMEM((2, HALF, LEG, TILE), bf),
            pltpu.VMEM((2, HALF, LEG, TILE), bf),
            pltpu.VMEM((2, 40, TILE), f32),
            pltpu.VMEM((40, TILE), f32),
            pltpu.SMEM((2, 40, TILE), f32),
            dma((HALF,)), dma((HALF,)), dma((HALF,)), dma((HALF,)), dma((HALF,)), dma((HALF,)), dma((3,)),
            dma((70,)), dma((70,)), dma((HALF,)), dma((HALF,)), dma((HALF,)),
            dma((HALF,)), dma((HALF,)), dma((HALF,)), dma((3, HALF)), dma((HALF,)), dma((HALF,)), dma((HALF,)), dma((HALF,)), dma((3, HALF)),
            dma((2, HALF)), dma((2, HALF)), dma((2, HALF)), dma((2, HALF)), dma((2, HALF)), dma((2, HALF)), dma((2, HALF)), dma((2, HALF)),
        ],
        compiler_params=pltpu.CompilerParams(
            collective_id=0, has_side_effects=True, vmem_limit_bytes=60 * 1024 * 1024
        ),
        cost_estimate=pl.CostEstimate(flops=17_000_000_000, bytes_accessed=60_000_000, transcendentals=0),
    )(amplitudes, integrals, pair_lists, pair_counts)
    ten = pl.BlockSpec((1, CHIP, TILE, TILE), lambda i: (i, 0, 0, 0))
    return pl.pallas_call(
        finish,
        grid=(HALF,),
        out_shape=tiles,
        in_specs=[ten, pl.BlockSpec((1, 2, PACK, TILE), lambda i: (i, 0, 0, 0))],
        out_specs=ten,
        compiler_params=pltpu.CompilerParams(vmem_limit_bytes=60 * 1024 * 1024),
    )(direct, mirror)


def solution(mesh):
    placed = (
        P("row", None, None, None),
        P("row", "col", None, None),
        P("row", "col", None),
        P("row", "col"),
    )
    return jax.shard_map(
        on_device,
        mesh=mesh,
        in_specs=placed,
        out_specs=P("row", "col", None, None),
        check_vma=False,
    )
```

```python
import functools

import jax
import jax.numpy as jnp
from jax import lax
from jax.experimental import pallas as pl
from jax.experimental.pallas import tpu as pltpu
from jax.sharding import PartitionSpec as P

MESH = pl.DeviceIdType.MESH
TILE = 128
O = 80
HALF = 5
CHIP = 10
Y_FIRST = ((1, 1, 1, 1, 1), (0, 0, 0, 0, 0))
PACK = HALF * TILE + 32
LEG = PACK // 2
SIGNS = (1, -1)
TOP = 2.0**15
Y, BACK, FRONT, FAR, BACK_Y, FRONT_Y, FAR_Y = range(7)


def kernel(
    amp, integ, lists, counts, direct, mirror,
    tv, wv, cyc, code, via_y, via_z, via_s, via_e, mine_v, mv, ms,
    own_sem, pair_send, pair_recv, t_own, t_send, t_recv, m_sem,
    g_send, g_recv, d_own, d_send, d_recv,
    y_send, y_recv, z_send, z_recv, a_send, a_recv, b_send, b_recv, c_send,
    s_send, s_recv, sa_send, sa_recv, e_send, e_recv, e1_send, eb_recv,
):
    row, col = lax.axis_index("row"), lax.axis_index("col")
    z, y, c = row // 4, (row // 2) % 2, row % 2
    chip = row // 2
    other = 1 - c
    sibling = (row + 1 - 2 * c, col)
    y_dev = (row + 2 - 4 * y, col)
    up = (lax.rem(row + 4, 16), col)
    down = (lax.rem(row + 12, 16), col)
    x, y_hi = col // 2, col % 2
    delta = lax.rem(z - x + 4, 4)

    def at(px, lo, hi, pz):
        return (pz * 4 + lo * 2 + c, px * 2 + hi)

    crossing = y != y_hi
    diagonal = delta == 0
    turned = lax.rem(delta, 2) == 1
    across = delta == 2
    sign = jnp.where(delta == 3, 1, -1)
    side = jnp.where(delta == 3, 0, 1)
    stays = jnp.logical_and(diagonal, jnp.logical_not(crossing))
    swapped = at(x, y_hi, y, z)
    flipped = at(z, y, y_hi, x)
    corner = at(x, y, y_hi, x)

    def block(dz, dy):
        return lax.rem(z + dz + 4, 4) * 2 + (y if dy == 0 else 1 - y)

    def near_x(step):
        return at(lax.rem(x + step + 4, 4), y, y_hi, z)

    def aslant(step, cross):
        lo, hi = (y_hi, y) if cross else (y, y_hi)
        return at(lax.rem(x + step + 4, 4), lo, hi, lax.rem(z + step + 4, 4))

    barrier = pltpu.get_barrier_semaphore()

    def greet(device):
        pl.semaphore_signal(barrier, inc=1, device_id=device, device_id_type=MESH)

    for device in (sibling, y_dev, up, down):
        greet(device)

    @pl.when(crossing)
    def _():
        greet(swapped)

    @pl.when(turned)
    def _():
        greet(flipped)
        greet(at(z, y_hi, y, z))
        greet(near_x(sign))
        greet(aslant(sign, True))
        greet(aslant(-sign, True))

    @pl.when(across)
    def _():
        for step in SIGNS:
            greet(near_x(step))
            greet(aslant(step, False))

    @pl.when(jnp.logical_and(across, crossing))
    def _():
        for step in SIGNS:
            greet(aslant(step, True))

    @pl.when(diagonal)
    def _():
        for step in (1, 3):
            greet(at(lax.rem(x + step, 4), y_hi, y, z))

    peers = (
        4 + jnp.where(crossing, 1, 0) + jnp.where(turned, 5, jnp.where(across, jnp.where(crossing, 6, 4), 2))
    )
    pl.semaphore_wait(barrier, peers)

    def remote(src, dst, send, recv, device):
        return pltpu.make_async_remote_copy(
            src_ref=src, dst_ref=dst, send_sem=send, recv_sem=recv, device_id=device, device_id_type=MESH
        )

    mine = pl.ds(chip * CHIP + c * HALF, HALF)
    theirs = pl.ds(chip * CHIP + other * HALF, HALF)
    own_w = [pltpu.make_async_copy(integ.at[:, c * HALF + j], wv.at[j, mine], own_sem.at[j]) for j in range(HALF)]
    pair_w = [
        remote(integ.at[:, other * HALF + j], wv.at[j, mine], pair_send.at[j], pair_recv.at[j], sibling)
        for j in range(HALF)
    ]
    for j in range(HALF):
        own_w[j].start()
        pair_w[j].start()

    mask_pair = remote(mine_v.at[other], mv, m_sem.at[0], m_sem.at[1], sibling)
    mask_own = pltpu.make_async_copy(mine_v.at[c], ms.at[c], m_sem.at[2])

    def make_mask():
        count_rows = counts[...]
        slots = lists.shape[2]
        eye = lax.broadcasted_iota(jnp.int32, (CHIP, CHIP), 0) == lax.broadcasted_iota(jnp.int32, (CHIP, CHIP), 1)
        slot_ids = lax.broadcasted_iota(jnp.int32, (CHIP, slots), 1)
        labels = lax.broadcasted_iota(jnp.int32, (CHIP, TILE), 1)
        for i in range(HALF):
            per_pair = jnp.broadcast_to(count_rows[i : i + 1], (CHIP, CHIP))
            count = jnp.sum(jnp.where(eye, per_pair, 0), axis=1, keepdims=True)
            kept = jnp.where(slot_ids < count, lists[i], -1)
            live = jnp.zeros((CHIP, TILE), jnp.float32)
            for s in range(slots):
                live = jnp.where(kept[:, s : s + 1] == labels, 1.0, live)
            for half in range(2):
                mine_v[half, i * 8 : i * 8 + HALF] = live[half * HALF : (half + 1) * HALF]

    def piece(part, j, dz, dy):
        view = pl.ds(block(dz, dy) * CHIP + (c if part == 0 else other) * HALF, HALF)
        return wv.at[j, view]

    sends = []

    def send(part, j, dz, dy, name, device):
        ref = piece(part, j, dz, dy)
        slot = (j * 2 + part) * 7 + name
        src = integ.at[:, c * HALF + j] if part == 0 and (dz, dy) == (0, 0) else ref
        remote(src, ref, g_send.at[slot], g_recv.at[slot], device).start()
        sends.append((part, j, dz, dy, name, device))

    def sent(part, j, dz, dy, name, device):
        ref = piece(part, j, dz, dy)
        slot = (j * 2 + part) * 7 + name
        remote(ref, ref, g_send.at[slot], g_recv.at[slot], device).wait_send()

    def arrived(part, j, name):
        far = ahead(part, j)[2]
        dz, dy = {
            Y: (0, 1), BACK: (-far, 0), FRONT: (far, 0), FAR: (2, 0),
            BACK_Y: (-far, 1), FRONT_Y: (far, 1), FAR_Y: (2, 1),
        }[name]
        ref = piece(part, j, dz, dy)
        slot = (j * 2 + part) * 7 + name
        remote(ref, ref, g_send.at[slot], g_recv.at[slot], y_dev).wait_recv()

    def ahead(part, j):
        return (up, down, 1) if (part + j) % 2 == 0 else (down, up, -1)

    def own(part, j):
        front, back, far = ahead(part, j)
        if part == 1:
            pair_w[j].wait_recv()
        send(part, j, 0, 0, BACK, front)
        send(part, j, 0, 0, FRONT, back)
        send(part, j, 0, 0, Y, y_dev)

    def first(part, j):
        front, back, far = ahead(part, j)
        if Y_FIRST[part][j]:
            arrived(part, j, Y)
            send(part, j, 0, 1, BACK_Y, front)
            send(part, j, 0, 1, FRONT_Y, back)
            arrived(part, j, BACK)
            send(part, j, -far, 0, FAR, front)
        else:
            arrived(part, j, BACK)
            send(part, j, -far, 0, FAR, front)
            send(part, j, -far, 0, BACK_Y, y_dev)
            arrived(part, j, FRONT)
            send(part, j, far, 0, FRONT_Y, y_dev)

    def second(part, j):
        front, back, far = ahead(part, j)
        if Y_FIRST[part][j]:
            arrived(part, j, BACK_Y)
            send(part, j, -far, 1, FAR_Y, front)
        else:
            arrived(part, j, FAR)
            send(part, j, 2, 0, FAR_Y, y_dev)

    def near(j):
        own_w[j].wait()
        for part in range(2):
            arrived(part, j, FRONT if Y_FIRST[part][j] else Y)

    def rest(j):
        for part in range(2):
            for name in (FRONT_Y, FAR) if Y_FIRST[part][j] else (BACK_Y, FRONT_Y):
                arrived(part, j, name)

    def last(j):
        for part in range(2):
            arrived(part, j, FAR_Y)

    def stage0(j):
        own(0, j)
        own(1, j)

    def stage1(j):
        first(0, j)
        first(1, j)

    def stage2(j):
        second(0, j)
        second(1, j)

    near_places = ((0, 0), (0, 1), (1, 0), (-1, 0))
    rest_places = ((1, 1), (-1, 1), (2, 0))
    last_places = ((2, 1),)

    def contract(j, places, i_from, i_to, final, hooks):
        starts = [block(dz, dy) * CHIP for dz, dy in places]
        labels = [start + k for start in starts for k in range(CHIP)]
        opening = places[0] == (0, 0)

        def one(i, scales):
            for step, hook in hooks.items():
                pl.when(i == step)(hook)
            left = jnp.concatenate([tv[i, k] for k in labels], axis=1)
            right = jnp.concatenate(
                [
                    wv[j, k]
                    * jnp.full((TILE, TILE), ms[i // HALF, lax.rem(i, HALF) * 8 + j, k], jnp.float32).astype(jnp.bfloat16)
                    for k in labels
                ],
                axis=0,
            )
            tile = jnp.dot(left, right, preferred_element_type=jnp.float32)
            if not opening:
                tile = tile + cyc[j, i]
            if final:
                n = i - i_from
                packed, scale = coded(tile.T)
                code[j, i_from // HALF, pl.ds(pl.multiple_of(n * TILE, TILE), TILE)] = packed
                scales = jnp.where(rows == n, scale[:8], scales)
            cyc[j, i] = tile
            return scales

        rows = lax.broadcasted_iota(jnp.int32, (8, TILE), 0)
        scales = lax.fori_loop(i_from, i_to, one, jnp.zeros((8, TILE), jnp.float32))
        if final:
            code[j, i_from // HALF, HALF * TILE : PACK] = jnp.concatenate([scales] * 4, axis=0).astype(jnp.bfloat16)

    def begin(j, hooks):
        contract(j, near_places, 0, CHIP, False, hooks)

    def carry_on(j, hooks):
        contract(j, rest_places, 0, CHIP, False, hooks)

    def end(j, places, hooks):
        for half in range(2):
            contract(j, places, half * HALF, (half + 1) * HALF, True, hooks)
            mirror_send(j, half)
            if j == HALF - 1 and half == 0:
                mirror_last(j - 1)
        hand_out(j)

    def mirror_half(j, half):
        return mirror.at[j, half]

    def to_y(j):
        return remote(code.at[j, 0], via_y.at[j], y_send.at[j], y_recv.at[j], swapped)

    def to_corner(j):
        slot = lax.rem(delta + 3, 4)
        return remote(code.at[j, 1], via_z.at[slot, j], z_send.at[j], z_recv.at[slot, j], corner)

    def straight(j, half, device):
        send_sem, recv_sem = (a_send, a_recv) if half == 0 else (b_send, b_recv)
        return remote(code.at[j, half], mirror_half(j, half), send_sem.at[j], recv_sem.at[j], device)

    def local(j, half):
        send_sem = a_send if half == 0 else b_send
        return pltpu.make_async_copy(code.at[j, half], mirror_half(j, half), send_sem.at[j])

    def second_a(j):
        return remote(via_y.at[j], mirror_half(j, 0), a_send.at[j], a_recv.at[j], flipped)

    def second_b(j, step):
        device = at(lax.rem(x + step, 4), y_hi, y, z)
        return remote(via_z.at[step - 1, j], mirror_half(j, 1), c_send.at[step - 1, j], b_recv.at[j], device)

    def leg(d):
        return pl.ds(d * LEG, LEG)

    def slant_out(j, d):
        return remote(
            code.at[j, 0, leg(d)], via_s.at[d, j], s_send.at[d, j], s_recv.at[d, j], aslant(SIGNS[d], True)
        )

    def slant_in(j, d):
        return remote(
            via_s.at[d, j], mirror.at[j, 0, leg(d)], sa_send.at[d, j], sa_recv.at[d, j], aslant(SIGNS[d], False)
        )

    def edge_out(j, d):
        return remote(
            code.at[j, 1, leg(d)], via_e.at[0, j], e_send.at[d, j], e_recv.at[0, j], up if d == 0 else down
        )

    def edge_mid(j):
        return remote(via_e.at[0, j], via_e.at[1, j], e1_send.at[0, j], e_recv.at[1, j], aslant(sign, True))

    def edge_in(j):
        rows = pl.ds(pl.multiple_of(side * LEG, 16), LEG)
        return remote(via_e.at[1, j], mirror.at[j, 1, rows], e1_send.at[1, j], eb_recv.at[side, j], near_x(sign))

    both = jnp.logical_and(crossing, turned)
    only_cross = jnp.logical_and(crossing, diagonal)
    only_turn = jnp.logical_and(jnp.logical_not(crossing), turned)

    def mirror_send(j, half):
        if half == 0:
            pl.when(both)(lambda: to_y(j).start())
            pl.when(only_turn)(lambda: straight(j, 0, flipped).start())
        else:
            pl.when(turned)(lambda: to_corner(j).start())
        pl.when(only_cross)(lambda: straight(j, half, swapped).start())
        pl.when(stays)(lambda: local(j, half).start())

        @pl.when(across)
        def _():
            for d in range(2):
                (slant_out if half == 0 else edge_out)(j, d).start()

    def mirror_relay(j):
        @pl.when(both)
        def _():
            to_y(j).wait_recv()
            second_a(j).start()

        @pl.when(diagonal)
        def _():
            for step in (1, 3):
                remote(code.at[j, 1], via_z.at[step - 1, j], z_send.at[j], z_recv.at[step - 1, j], sibling).wait_recv()
                second_b(j, step).start()

        @pl.when(across)
        def _():
            for d in range(2):
                slant_out(j, d).wait_recv()
                slant_in(j, d).start()

        @pl.when(turned)
        def _():
            edge_out(j, 0).wait_recv()
            edge_mid(j).start()

    def mirror_last(j):
        @pl.when(turned)
        def _():
            edge_mid(j).wait_recv()
            edge_in(j).start()

    def mirror_wait(j):
        @pl.when(across)
        def _():
            for d in range(2):
                slant_out(j, d).wait_send()
                slant_in(j, d).wait()
                edge_out(j, d).wait_send()
                remote(
                    code.at[j, 1, leg(d)], mirror.at[j, 1, leg(d)], e_send.at[d, j], eb_recv.at[d, j], sibling
                ).wait_recv()

        @pl.when(turned)
        def _():
            edge_mid(j).wait_send()
            edge_in(j).wait_send()

        @pl.when(both)
        def _():
            to_y(j).wait_send()
            second_a(j).wait()

        @pl.when(only_turn)
        def _():
            straight(j, 0, flipped).wait()

        @pl.when(turned)
        def _():
            to_corner(j).wait_send()
            straight(j, 1, flipped).wait_recv()

        @pl.when(only_cross)
        def _():
            straight(j, 0, swapped).wait()
            straight(j, 1, swapped).wait()

        @pl.when(stays)
        def _():
            local(j, 0).wait()
            local(j, 1).wait()

        @pl.when(diagonal)
        def _():
            for step in (1, 3):
                second_b(j, step).wait_send()

    finals = []

    def hand_out(j):
        keep = pltpu.make_async_copy(cyc.at[j, pl.ds(c * HALF, HALF)], direct.at[:, c * HALF + j], d_own.at[j])
        keep.start()
        pair = remote(
            cyc.at[j, pl.ds(other * HALF, HALF)], direct.at[:, c * HALF + j], d_send.at[j], d_recv.at[j], sibling
        )
        pair.start()

        finals.append((keep, pair))

    t_local = [pltpu.make_async_copy(amp.at[i], tv.at[c * HALF + i], t_own.at[i]) for i in range(HALF)]
    t_pair = [remote(amp.at[i], tv.at[c * HALF + i], t_send.at[i], t_recv.at[i], sibling) for i in range(HALF)]

    stage0(0)
    for i in range(HALF):
        t_local[i].start()
        t_pair[i].start()
    stage0(1)
    make_mask()
    mask_pair.start()
    mask_own.start()
    stage1(0)
    stage2(0)
    mask_pair.wait()
    mask_own.wait()
    mask_theirs = pltpu.make_async_copy(mv, ms.at[other], m_sem.at[2])
    mask_theirs.start()
    mask_theirs.wait()
    for i in range(HALF):
        t_local[i].wait()
        t_pair[i].wait()
    stage1(1)
    stage0(2)
    near(0)
    begin(0, {})
    rest(0)
    last(0)
    end(0, rest_places + last_places, {})
    stage2(1)
    stage1(2)
    stage0(3)
    near(1)
    begin(1, {})
    mirror_relay(0)
    rest(1)
    last(1)
    end(1, rest_places + last_places, {})
    mirror_last(0)
    stage2(2)
    stage1(3)
    stage0(4)
    near(2)
    begin(2, {})
    mirror_relay(1)
    rest(2)
    last(2)
    end(2, rest_places + last_places, {})
    mirror_last(1)
    stage2(3)
    stage1(4)
    near(3)
    begin(3, {})
    mirror_relay(2)
    rest(3)
    last(3)
    end(3, rest_places + last_places, {})
    mirror_last(2)
    stage2(4)
    near(4)
    begin(4, {})
    mirror_relay(3)
    rest(4)
    last(4)
    end(4, rest_places + last_places, {})
    mirror_relay(4)
    mirror_last(4)

    for way in sends:
        sent(*way)
    for copy in pair_w:
        copy.wait_send()
    for keep, pair in finals:
        keep.wait()
        pair.wait()
    for j in range(HALF):
        mirror_wait(j)


def coded(tile):
    largest = jnp.max(jnp.max(jnp.abs(tile), axis=0, keepdims=True), axis=1, keepdims=True)
    scale = jnp.broadcast_to(jnp.maximum(largest, 2.0**-100), (16, TILE)).astype(jnp.bfloat16).astype(jnp.float32)
    value = tile * (TOP / scale[:1])
    square = value * value
    fourth = square * square
    eighth = fourth * fourth
    return jnp.where(value < 0, -eighth, eighth).astype(jnp.bfloat16), scale


def finish(direct, mirror, out):
    for half in range(2):
        scales = mirror[0, half, HALF * TILE : PACK].astype(jnp.float32) * (1 / TOP)
        for n in range(HALF):
            value = mirror[0, half, n * TILE : (n + 1) * TILE].astype(jnp.float32)
            inverse = lax.rsqrt(jnp.maximum(jnp.abs(value), 2.0**-126))
            quarter = lax.rsqrt(inverse)
            root = quarter * lax.rsqrt(quarter) * scales[n : n + 1]
            out[0, half * HALF + n] = direct[0, half * HALF + n] + jnp.where(value < 0, -root, root)


def on_device(amplitudes, integrals, pair_lists, pair_counts):
    bf, f32 = jnp.bfloat16, jnp.float32
    dma = pltpu.SemaphoreType.DMA
    tiles = jax.ShapeDtypeStruct((HALF, CHIP, TILE, TILE), f32)
    anywhere = pl.BlockSpec(memory_space=pl.ANY)
    direct, mirror = pl.pallas_call(
        kernel,
        out_shape=(tiles, jax.ShapeDtypeStruct((HALF, 2, PACK, TILE), bf)),
        in_specs=[anywhere] * 2 + [pl.BlockSpec(memory_space=pltpu.VMEM)] * 2,
        out_specs=(anywhere, anywhere),
        scratch_shapes=[
            pltpu.VMEM((CHIP, O, TILE, TILE), bf),
            pltpu.VMEM((HALF, O, TILE, TILE), bf),
            pltpu.VMEM((HALF, CHIP, TILE, TILE), f32),
            pltpu.VMEM((HALF, 2, PACK, TILE), bf),
            pltpu.VMEM((HALF, PACK, TILE), bf),
            pltpu.VMEM((3, HALF, PACK, TILE), bf),
            pltpu.VMEM((2, HALF, LEG, TILE), bf),
            pltpu.VMEM((2, HALF, LEG, TILE), bf),
            pltpu.VMEM((2, 40, TILE), f32),
            pltpu.VMEM((40, TILE), f32),
            pltpu.SMEM((2, 40, TILE), f32),
            dma((HALF,)), dma((HALF,)), dma((HALF,)), dma((HALF,)), dma((HALF,)), dma((HALF,)), dma((3,)),
            dma((70,)), dma((70,)), dma((HALF,)), dma((HALF,)), dma((HALF,)),
            dma((HALF,)), dma((HALF,)), dma((HALF,)), dma((3, HALF)), dma((HALF,)), dma((HALF,)), dma((HALF,)), dma((HALF,)), dma((3, HALF)),
            dma((2, HALF)), dma((2, HALF)), dma((2, HALF)), dma((2, HALF)), dma((2, HALF)), dma((2, HALF)), dma((2, HALF)), dma((2, HALF)),
        ],
        compiler_params=pltpu.CompilerParams(
            collective_id=0, has_side_effects=True, vmem_limit_bytes=60 * 1024 * 1024
        ),
        cost_estimate=pl.CostEstimate(flops=17_000_000_000, bytes_accessed=60_000_000, transcendentals=0),
    )(amplitudes, integrals, pair_lists, pair_counts)
    ten = pl.BlockSpec((1, CHIP, TILE, TILE), lambda i: (i, 0, 0, 0))
    return pl.pallas_call(
        finish,
        grid=(HALF,),
        out_shape=tiles,
        in_specs=[ten, pl.BlockSpec((1, 2, PACK, TILE), lambda i: (i, 0, 0, 0))],
        out_specs=ten,
        compiler_params=pltpu.CompilerParams(vmem_limit_bytes=60 * 1024 * 1024),
    )(direct, mirror)


def solution(mesh):
    placed = (
        P("row", None, None, None),
        P("row", "col", None, None),
        P("row", "col", None),
        P("row", "col"),
    )
    return jax.shard_map(
        on_device,
        mesh=mesh,
        in_specs=placed,
        out_specs=P("row", "col", None, None),
        check_vma=False,
    )
```

```python
import functools

import jax
import jax.numpy as jnp
from jax import lax
from jax.experimental import pallas as pl
from jax.experimental.pallas import tpu as pltpu
from jax.sharding import PartitionSpec as P

MESH = pl.DeviceIdType.MESH
TILE = 128
O = 80
HALF = 5
CHIP = 10
Y_FIRST = ((1, 1, 1, 1, 1), (0, 0, 0, 0, 0))
PACK = HALF * TILE + 32
LEG = PACK // 2
SIGNS = (1, -1)
TOP = 2.0**15
Y, BACK, FRONT, FAR, BACK_Y, FRONT_Y, FAR_Y = range(7)


def kernel(
    amp, integ, lists, counts, direct, mirror,
    tv, wv, cyc, code, via_y, via_z, via_s, via_e, mine_v, mv, ms,
    own_sem, pair_send, pair_recv, t_own, t_send, t_recv, m_sem,
    g_send, g_recv, d_own, d_send, d_recv,
    y_send, y_recv, z_send, z_recv, a_send, a_recv, b_send, b_recv, c_send,
    s_send, s_recv, sa_send, sa_recv, e_send, e_recv, e1_send, eb_recv,
):
    row, col = lax.axis_index("row"), lax.axis_index("col")
    z, y, c = row // 4, (row // 2) % 2, row % 2
    chip = row // 2
    other = 1 - c
    sibling = (row + 1 - 2 * c, col)
    y_dev = (row + 2 - 4 * y, col)
    up = (lax.rem(row + 4, 16), col)
    down = (lax.rem(row + 12, 16), col)
    x, y_hi = col // 2, col % 2
    delta = lax.rem(z - x + 4, 4)

    def at(px, lo, hi, pz):
        return (pz * 4 + lo * 2 + c, px * 2 + hi)

    crossing = y != y_hi
    diagonal = delta == 0
    turned = lax.rem(delta, 2) == 1
    across = delta == 2
    sign = jnp.where(delta == 3, 1, -1)
    side = jnp.where(delta == 3, 0, 1)
    stays = jnp.logical_and(diagonal, jnp.logical_not(crossing))
    swapped = at(x, y_hi, y, z)
    flipped = at(z, y, y_hi, x)
    corner = at(x, y, y_hi, x)

    def block(dz, dy):
        return lax.rem(z + dz + 4, 4) * 2 + (y if dy == 0 else 1 - y)

    def near_x(step):
        return at(lax.rem(x + step + 4, 4), y, y_hi, z)

    def aslant(step, cross):
        lo, hi = (y_hi, y) if cross else (y, y_hi)
        return at(lax.rem(x + step + 4, 4), lo, hi, lax.rem(z + step + 4, 4))

    barrier = pltpu.get_barrier_semaphore()

    def greet(device):
        pl.semaphore_signal(barrier, inc=1, device_id=device, device_id_type=MESH)

    for device in (sibling, y_dev, up, down):
        greet(device)

    @pl.when(crossing)
    def _():
        greet(swapped)

    @pl.when(turned)
    def _():
        greet(flipped)
        greet(at(z, y_hi, y, z))
        greet(near_x(sign))
        greet(aslant(sign, True))
        greet(aslant(-sign, True))

    @pl.when(across)
    def _():
        for step in SIGNS:
            greet(near_x(step))
            greet(aslant(step, False))

    @pl.when(jnp.logical_and(across, crossing))
    def _():
        for step in SIGNS:
            greet(aslant(step, True))

    @pl.when(diagonal)
    def _():
        for step in (1, 3):
            greet(at(lax.rem(x + step, 4), y_hi, y, z))

    peers = (
        4 + jnp.where(crossing, 1, 0) + jnp.where(turned, 5, jnp.where(across, jnp.where(crossing, 6, 4), 2))
    )
    def make_mask():
        count_rows = counts[...]
        slots = lists.shape[2]
        eye = lax.broadcasted_iota(jnp.int32, (CHIP, CHIP), 0) == lax.broadcasted_iota(jnp.int32, (CHIP, CHIP), 1)
        slot_ids = lax.broadcasted_iota(jnp.int32, (CHIP, slots), 1)
        labels = lax.broadcasted_iota(jnp.int32, (CHIP, TILE), 1)
        for i in range(HALF):
            per_pair = jnp.broadcast_to(count_rows[i : i + 1], (CHIP, CHIP))
            count = jnp.sum(jnp.where(eye, per_pair, 0), axis=1, keepdims=True)
            kept = jnp.where(slot_ids < count, lists[i], -1)
            live = jnp.zeros((CHIP, TILE), jnp.float32)
            for s in range(slots):
                live = jnp.where(kept[:, s : s + 1] == labels, 1.0, live)
            for half in range(2):
                mine_v[half, i * 8 : i * 8 + HALF] = live[half * HALF : (half + 1) * HALF]

    make_mask()
    pl.semaphore_wait(barrier, peers)

    def remote(src, dst, send, recv, device):
        return pltpu.make_async_remote_copy(
            src_ref=src, dst_ref=dst, send_sem=send, recv_sem=recv, device_id=device, device_id_type=MESH
        )

    mine = pl.ds(chip * CHIP + c * HALF, HALF)
    theirs = pl.ds(chip * CHIP + other * HALF, HALF)
    own_w = [pltpu.make_async_copy(integ.at[:, c * HALF + j], wv.at[j, mine], own_sem.at[j]) for j in range(HALF)]
    pair_w = [
        remote(integ.at[:, other * HALF + j], wv.at[j, mine], pair_send.at[j], pair_recv.at[j], sibling)
        for j in range(HALF)
    ]
    for j in range(HALF):
        own_w[j].start()
        pair_w[j].start()

    mask_pair = remote(mine_v.at[other], mv, m_sem.at[0], m_sem.at[1], sibling)
    mask_own = pltpu.make_async_copy(mine_v.at[c], ms.at[c], m_sem.at[2])

    def piece(part, j, dz, dy):
        view = pl.ds(block(dz, dy) * CHIP + (c if part == 0 else other) * HALF, HALF)
        return wv.at[j, view]

    sends = []

    def send(part, j, dz, dy, name, device):
        ref = piece(part, j, dz, dy)
        slot = (j * 2 + part) * 7 + name
        src = integ.at[:, c * HALF + j] if part == 0 and (dz, dy) == (0, 0) else ref
        remote(src, ref, g_send.at[slot], g_recv.at[slot], device).start()
        sends.append((part, j, dz, dy, name, device))

    def sent(part, j, dz, dy, name, device):
        ref = piece(part, j, dz, dy)
        slot = (j * 2 + part) * 7 + name
        remote(ref, ref, g_send.at[slot], g_recv.at[slot], device).wait_send()

    def arrived(part, j, name):
        far = ahead(part, j)[2]
        dz, dy = {
            Y: (0, 1), BACK: (-far, 0), FRONT: (far, 0), FAR: (2, 0),
            BACK_Y: (-far, 1), FRONT_Y: (far, 1), FAR_Y: (2, 1),
        }[name]
        ref = piece(part, j, dz, dy)
        slot = (j * 2 + part) * 7 + name
        remote(ref, ref, g_send.at[slot], g_recv.at[slot], y_dev).wait_recv()

    def ahead(part, j):
        return (up, down, 1) if (part + j) % 2 == 0 else (down, up, -1)

    def own(part, j):
        front, back, far = ahead(part, j)
        if part == 1:
            pair_w[j].wait_recv()
        send(part, j, 0, 0, BACK, front)
        send(part, j, 0, 0, FRONT, back)
        send(part, j, 0, 0, Y, y_dev)

    def first(part, j):
        front, back, far = ahead(part, j)
        if Y_FIRST[part][j]:
            arrived(part, j, Y)
            send(part, j, 0, 1, BACK_Y, front)
            send(part, j, 0, 1, FRONT_Y, back)
            arrived(part, j, BACK)
            send(part, j, -far, 0, FAR, front)
        else:
            arrived(part, j, BACK)
            send(part, j, -far, 0, FAR, front)
            send(part, j, -far, 0, BACK_Y, y_dev)
            arrived(part, j, FRONT)
            send(part, j, far, 0, FRONT_Y, y_dev)

    def second(part, j):
        front, back, far = ahead(part, j)
        if Y_FIRST[part][j]:
            arrived(part, j, BACK_Y)
            send(part, j, -far, 1, FAR_Y, front)
        else:
            arrived(part, j, FAR)
            send(part, j, 2, 0, FAR_Y, y_dev)

    def near(j):
        own_w[j].wait()
        for part in range(2):
            arrived(part, j, FRONT if Y_FIRST[part][j] else Y)

    def rest(j):
        for part in range(2):
            for name in (FRONT_Y, FAR) if Y_FIRST[part][j] else (BACK_Y, FRONT_Y):
                arrived(part, j, name)

    def last(j):
        for part in range(2):
            arrived(part, j, FAR_Y)

    def stage0(j):
        own(0, j)
        own(1, j)

    def stage1(j):
        first(0, j)
        first(1, j)

    def stage2(j):
        second(0, j)
        second(1, j)

    near_places = ((0, 0), (0, 1), (1, 0), (-1, 0))
    rest_places = ((1, 1), (-1, 1), (2, 0))
    last_places = ((2, 1),)

    def contract(j, places, i_from, i_to, final, hooks):
        starts = [block(dz, dy) * CHIP for dz, dy in places]
        labels = [start + k for start in starts for k in range(CHIP)]
        opening = places[0] == (0, 0)

        def one(i, scales):
            for step, hook in hooks.items():
                pl.when(i == step)(hook)
            left = jnp.concatenate([tv[i, k] for k in labels], axis=1)
            right = jnp.concatenate(
                [
                    wv[j, k]
                    * jnp.full((TILE, TILE), ms[i // HALF, lax.rem(i, HALF) * 8 + j, k], jnp.float32).astype(jnp.bfloat16)
                    for k in labels
                ],
                axis=0,
            )
            tile = jnp.dot(left, right, preferred_element_type=jnp.float32)
            if not opening:
                tile = tile + cyc[j, i]
            if final:
                n = i - i_from
                packed, scale = coded(tile.T)
                code[j, i_from // HALF, pl.ds(pl.multiple_of(n * TILE, TILE), TILE)] = packed
                scales = jnp.where(rows == n, scale[:8], scales)
            cyc[j, i] = tile
            return scales

        rows = lax.broadcasted_iota(jnp.int32, (8, TILE), 0)
        scales = lax.fori_loop(i_from, i_to, one, jnp.zeros((8, TILE), jnp.float32))
        if final:
            code[j, i_from // HALF, HALF * TILE : PACK] = jnp.concatenate([scales] * 4, axis=0).astype(jnp.bfloat16)

    def begin(j, hooks):
        contract(j, near_places, 0, CHIP, False, hooks)

    def carry_on(j, hooks):
        contract(j, rest_places, 0, CHIP, False, hooks)

    def end(j, places, hooks):
        for half in range(2):
            contract(j, places, half * HALF, (half + 1) * HALF, True, hooks)
            mirror_send(j, half)
            if j == HALF - 1 and half == 0:
                mirror_last(j - 1)
        hand_out(j)

    def mirror_half(j, half):
        return mirror.at[j, half]

    def to_y(j):
        return remote(code.at[j, 0], via_y.at[j], y_send.at[j], y_recv.at[j], swapped)

    def to_corner(j):
        slot = lax.rem(delta + 3, 4)
        return remote(code.at[j, 1], via_z.at[slot, j], z_send.at[j], z_recv.at[slot, j], corner)

    def straight(j, half, device):
        send_sem, recv_sem = (a_send, a_recv) if half == 0 else (b_send, b_recv)
        return remote(code.at[j, half], mirror_half(j, half), send_sem.at[j], recv_sem.at[j], device)

    def local(j, half):
        send_sem = a_send if half == 0 else b_send
        return pltpu.make_async_copy(code.at[j, half], mirror_half(j, half), send_sem.at[j])

    def second_a(j):
        return remote(via_y.at[j], mirror_half(j, 0), a_send.at[j], a_recv.at[j], flipped)

    def second_b(j, step):
        device = at(lax.rem(x + step, 4), y_hi, y, z)
        return remote(via_z.at[step - 1, j], mirror_half(j, 1), c_send.at[step - 1, j], b_recv.at[j], device)

    def leg(d):
        return pl.ds(d * LEG, LEG)

    def slant_out(j, d):
        return remote(
            code.at[j, 0, leg(d)], via_s.at[d, j], s_send.at[d, j], s_recv.at[d, j], aslant(SIGNS[d], True)
        )

    def slant_in(j, d):
        return remote(
            via_s.at[d, j], mirror.at[j, 0, leg(d)], sa_send.at[d, j], sa_recv.at[d, j], aslant(SIGNS[d], False)
        )

    def edge_out(j, d):
        return remote(
            code.at[j, 1, leg(d)], via_e.at[0, j], e_send.at[d, j], e_recv.at[0, j], up if d == 0 else down
        )

    def edge_mid(j):
        return remote(via_e.at[0, j], via_e.at[1, j], e1_send.at[0, j], e_recv.at[1, j], aslant(sign, True))

    def edge_in(j):
        rows = pl.ds(pl.multiple_of(side * LEG, 16), LEG)
        return remote(via_e.at[1, j], mirror.at[j, 1, rows], e1_send.at[1, j], eb_recv.at[side, j], near_x(sign))

    both = jnp.logical_and(crossing, turned)
    only_cross = jnp.logical_and(crossing, diagonal)
    only_turn = jnp.logical_and(jnp.logical_not(crossing), turned)

    def mirror_send(j, half):
        if half == 0:
            pl.when(both)(lambda: to_y(j).start())
            pl.when(only_turn)(lambda: straight(j, 0, flipped).start())
        else:
            pl.when(turned)(lambda: to_corner(j).start())
        pl.when(only_cross)(lambda: straight(j, half, swapped).start())
        pl.when(stays)(lambda: local(j, half).start())

        @pl.when(across)
        def _():
            for d in range(2):
                (slant_out if half == 0 else edge_out)(j, d).start()

    def mirror_relay(j):
        @pl.when(both)
        def _():
            to_y(j).wait_recv()
            second_a(j).start()

        @pl.when(diagonal)
        def _():
            for step in (1, 3):
                remote(code.at[j, 1], via_z.at[step - 1, j], z_send.at[j], z_recv.at[step - 1, j], sibling).wait_recv()
                second_b(j, step).start()

        @pl.when(across)
        def _():
            for d in range(2):
                slant_out(j, d).wait_recv()
                slant_in(j, d).start()

        @pl.when(turned)
        def _():
            edge_out(j, 0).wait_recv()
            edge_mid(j).start()

    def mirror_last(j):
        @pl.when(turned)
        def _():
            edge_mid(j).wait_recv()
            edge_in(j).start()

    def mirror_wait(j):
        @pl.when(across)
        def _():
            for d in range(2):
                slant_out(j, d).wait_send()
                slant_in(j, d).wait()
                edge_out(j, d).wait_send()
                remote(
                    code.at[j, 1, leg(d)], mirror.at[j, 1, leg(d)], e_send.at[d, j], eb_recv.at[d, j], sibling
                ).wait_recv()

        @pl.when(turned)
        def _():
            edge_mid(j).wait_send()
            edge_in(j).wait_send()

        @pl.when(both)
        def _():
            to_y(j).wait_send()
            second_a(j).wait()

        @pl.when(only_turn)
        def _():
            straight(j, 0, flipped).wait()

        @pl.when(turned)
        def _():
            to_corner(j).wait_send()
            straight(j, 1, flipped).wait_recv()

        @pl.when(only_cross)
        def _():
            straight(j, 0, swapped).wait()
            straight(j, 1, swapped).wait()

        @pl.when(stays)
        def _():
            local(j, 0).wait()
            local(j, 1).wait()

        @pl.when(diagonal)
        def _():
            for step in (1, 3):
                second_b(j, step).wait_send()

    finals = []

    def hand_out(j):
        keep = pltpu.make_async_copy(cyc.at[j, pl.ds(c * HALF, HALF)], direct.at[:, c * HALF + j], d_own.at[j])
        keep.start()
        pair = remote(
            cyc.at[j, pl.ds(other * HALF, HALF)], direct.at[:, c * HALF + j], d_send.at[j], d_recv.at[j], sibling
        )
        pair.start()

        finals.append((keep, pair))

    t_local = [pltpu.make_async_copy(amp.at[i], tv.at[c * HALF + i], t_own.at[i]) for i in range(HALF)]
    t_pair = [remote(amp.at[i], tv.at[c * HALF + i], t_send.at[i], t_recv.at[i], sibling) for i in range(HALF)]

    stage0(0)
    for i in range(HALF):
        t_local[i].start()
        t_pair[i].start()
    stage0(1)
    mask_pair.start()
    mask_own.start()
    stage1(0)
    stage2(0)
    mask_pair.wait()
    mask_own.wait()
    mask_theirs = pltpu.make_async_copy(mv, ms.at[other], m_sem.at[2])
    mask_theirs.start()
    mask_theirs.wait()
    for i in range(HALF):
        t_local[i].wait()
        t_pair[i].wait()
    stage1(1)
    stage0(2)
    near(0)
    begin(0, {})
    rest(0)
    last(0)
    end(0, rest_places + last_places, {})
    stage2(1)
    stage1(2)
    stage0(3)
    near(1)
    begin(1, {})
    mirror_relay(0)
    rest(1)
    last(1)
    end(1, rest_places + last_places, {})
    mirror_last(0)
    stage2(2)
    stage1(3)
    stage0(4)
    near(2)
    begin(2, {})
    mirror_relay(1)
    rest(2)
    last(2)
    end(2, rest_places + last_places, {})
    mirror_last(1)
    stage2(3)
    stage1(4)
    near(3)
    begin(3, {})
    mirror_relay(2)
    rest(3)
    last(3)
    end(3, rest_places + last_places, {})
    mirror_last(2)
    stage2(4)
    near(4)
    begin(4, {})
    mirror_relay(3)
    rest(4)
    last(4)
    end(4, rest_places + last_places, {})
    mirror_relay(4)
    mirror_last(4)

    for way in sends:
        sent(*way)
    for copy in pair_w:
        copy.wait_send()
    for keep, pair in finals:
        keep.wait()
        pair.wait()
    for j in range(HALF):
        mirror_wait(j)


def coded(tile):
    largest = jnp.max(jnp.max(jnp.abs(tile), axis=0, keepdims=True), axis=1, keepdims=True)
    scale = jnp.broadcast_to(jnp.maximum(largest, 2.0**-100), (16, TILE)).astype(jnp.bfloat16).astype(jnp.float32)
    value = tile * (TOP / scale[:1])
    square = value * value
    fourth = square * square
    eighth = fourth * fourth
    return jnp.where(value < 0, -eighth, eighth).astype(jnp.bfloat16), scale


def finish(direct, mirror, out):
    for half in range(2):
        scales = mirror[0, half, HALF * TILE : PACK].astype(jnp.float32) * (1 / TOP)
        for n in range(HALF):
            value = mirror[0, half, n * TILE : (n + 1) * TILE].astype(jnp.float32)
            inverse = lax.rsqrt(jnp.maximum(jnp.abs(value), 2.0**-126))
            quarter = lax.rsqrt(inverse)
            root = quarter * lax.rsqrt(quarter) * scales[n : n + 1]
            out[0, half * HALF + n] = direct[0, half * HALF + n] + jnp.where(value < 0, -root, root)


def on_device(amplitudes, integrals, pair_lists, pair_counts):
    bf, f32 = jnp.bfloat16, jnp.float32
    dma = pltpu.SemaphoreType.DMA
    tiles = jax.ShapeDtypeStruct((HALF, CHIP, TILE, TILE), f32)
    anywhere = pl.BlockSpec(memory_space=pl.ANY)
    direct, mirror = pl.pallas_call(
        kernel,
        out_shape=(tiles, jax.ShapeDtypeStruct((HALF, 2, PACK, TILE), bf)),
        in_specs=[anywhere] * 2 + [pl.BlockSpec(memory_space=pltpu.VMEM)] * 2,
        out_specs=(anywhere, anywhere),
        scratch_shapes=[
            pltpu.VMEM((CHIP, O, TILE, TILE), bf),
            pltpu.VMEM((HALF, O, TILE, TILE), bf),
            pltpu.VMEM((HALF, CHIP, TILE, TILE), f32),
            pltpu.VMEM((HALF, 2, PACK, TILE), bf),
            pltpu.VMEM((HALF, PACK, TILE), bf),
            pltpu.VMEM((3, HALF, PACK, TILE), bf),
            pltpu.VMEM((2, HALF, LEG, TILE), bf),
            pltpu.VMEM((2, HALF, LEG, TILE), bf),
            pltpu.VMEM((2, 40, TILE), f32),
            pltpu.VMEM((40, TILE), f32),
            pltpu.SMEM((2, 40, TILE), f32),
            dma((HALF,)), dma((HALF,)), dma((HALF,)), dma((HALF,)), dma((HALF,)), dma((HALF,)), dma((3,)),
            dma((70,)), dma((70,)), dma((HALF,)), dma((HALF,)), dma((HALF,)),
            dma((HALF,)), dma((HALF,)), dma((HALF,)), dma((3, HALF)), dma((HALF,)), dma((HALF,)), dma((HALF,)), dma((HALF,)), dma((3, HALF)),
            dma((2, HALF)), dma((2, HALF)), dma((2, HALF)), dma((2, HALF)), dma((2, HALF)), dma((2, HALF)), dma((2, HALF)), dma((2, HALF)),
        ],
        compiler_params=pltpu.CompilerParams(
            collective_id=0, has_side_effects=True, vmem_limit_bytes=60 * 1024 * 1024
        ),
        cost_estimate=pl.CostEstimate(flops=17_000_000_000, bytes_accessed=60_000_000, transcendentals=0),
    )(amplitudes, integrals, pair_lists, pair_counts)
    ten = pl.BlockSpec((1, CHIP, TILE, TILE), lambda i: (i, 0, 0, 0))
    return pl.pallas_call(
        finish,
        grid=(HALF,),
        out_shape=tiles,
        in_specs=[ten, pl.BlockSpec((1, 2, PACK, TILE), lambda i: (i, 0, 0, 0))],
        out_specs=ten,
        compiler_params=pltpu.CompilerParams(vmem_limit_bytes=60 * 1024 * 1024),
    )(direct, mirror)


def solution(mesh):
    placed = (
        P("row", None, None, None),
        P("row", "col", None, None),
        P("row", "col", None),
        P("row", "col"),
    )
    return jax.shard_map(
        on_device,
        mesh=mesh,
        in_specs=placed,
        out_specs=P("row", "col", None, None),
        check_vma=False,
    )
```
